256 devices in a mesh: gx: 4 (over y), gy: 8 (over z_lo, x), gz: 8 (over z_hi, core).
Axes of the slice: x: 4, y: 4, z: 8 (z_hi: 4, z_lo: 2; z = z_hi * 2 + z_lo), core: 2. Of those that a mesh axis runs over, the one named last changes fastest.
Arguments:
- unary_q: int32 [32, 64, 64, 128], P('gx', 'gy', 'gz'), may hold values from -127 to 127
- potential_q: int32 [128, 128], replicated, may hold values from -127 to 127
- belief_grad: bfloat16 [32, 64, 64, 128], P('gx', 'gy', 'gz'), may hold values from -6 to 6
Outputs:
- unary_grad: float32 [32, 64, 64, 128], P('gx', 'gy', 'gz')
- potential_grad: float32 [128, 128], replicated
The draws below stay inside these ranges and needn't reach their ends.
All inputs are finite; a program needn't handle non-finite values.
Results may differ from the reference program's by a relative error of at most 0.008.
Values may be sent and summed in bfloat16 or wider, within the bound.
A program may use at most 64 MiB of HBM per device.

```python
import math
import jax
import jax.numpy as jnp
from jax import lax

L = 128
ITERS = 3
NX = 32
NY = 64
NZ = 64
CELLS = 131072


def touch_ends(drawn, rng, smallest, top_value):
    longest = drawn.shape.index(max(drawn.shape))
    spots = []
    for shift in (0, 1):
        where = [jax.random.randint(jax.random.fold_in(rng, axis), (), 0, length) for axis, length in enumerate(drawn.shape)]
        where[longest] = (where[longest] + shift) % drawn.shape[longest]
        spots.append(tuple(where))
    return drawn.at[spots[0]].set(smallest).at[spots[1]].set(top_value)


def block_scale(key, shape, cuts, smallest, largest):
    def one(dim, parts):
        steps = jax.random.uniform(jax.random.fold_in(jax.random.fold_in(key, 6), dim), (parts,), jnp.float32, smallest / len(cuts), largest / len(cuts))
        return jnp.repeat(jnp.exp(steps), shape[dim] // parts).reshape((-1,) + (1,) * (len(shape) - dim - 1))

    loudness = one(*cuts[0])
    for cut in cuts[1:]:
        loudness = loudness * one(*cut)
    return loudness


def noise(stream_key, shape, width, reach, pieces=(), held_as=jnp.bfloat16):
    values = width * jax.random.normal(stream_key, shape, jnp.float32)
    if pieces:
        values = values * block_scale(stream_key, shape, pieces, -0.22, 0.18)
    return jnp.clip(values, -reach, reach).astype(held_as)


def setup_inputs(seed: int = 0) -> dict:
    streams_of = jax.random.split(jax.random.key(seed), 4)
    unary_q = touch_ends(jax.random.randint(streams_of[0], (NX, NY, NZ, L), -127, 128), jax.random.fold_in(streams_of[0], 1), -127, 127).astype(jnp.int32)
    potential_q = touch_ends(jax.random.randint(streams_of[1], (L, L), -127, 128), jax.random.fold_in(streams_of[1], 1), -127, 127).astype(jnp.int32)
    belief_grad = noise(streams_of[2], (NX, NY, NZ, L), 1.0, 6.0, ((0, 4), (1, 8), (2, 8)))
    return {"unary_q": unary_q, "potential_q": potential_q, "belief_grad": belief_grad}


OPPOSITE = (1, 0, 3, 2, 5, 4)

def layers(values, spatial, begin_at, end_at):
    return lax.slice_in_dim(values, begin_at, end_at, axis=spatial)

def shift_in(values, spatial, forward, fill_value):
    extent = values.shape[spatial]
    border = jnp.full_like(layers(values, spatial, 0, 1), fill_value)
    if forward:
        return jnp.concatenate([border, layers(values, spatial, 0, extent - 1)], axis=spatial)
    return jnp.concatenate([layers(values, spatial, 1, extent), border], axis=spatial)

def shift_back(values, spatial, forward):
    extent = values.shape[spatial]
    border = jnp.zeros_like(layers(values, spatial, 0, 1))
    if forward:
        return jnp.concatenate([layers(values, spatial, 1, extent), border], axis=spatial)
    return jnp.concatenate([border, layers(values, spatial, 0, extent - 1)], axis=spatial)

def project(operand, table):
    out_shape = operand.shape[:-1] + (table.shape[1],)
    result = jnp.dot(operand.reshape(-1, operand.shape[-1]), table, preferred_element_type=jnp.float32)
    return result.reshape(out_shape)

def cell_product(unary_factor, incoming):
    product = unary_factor
    for direction in range(6):
        product = product * incoming[direction].astype(jnp.float32)
    return product

def reference(unary_q, potential_q, belief_grad):
    unary_factor = jnp.exp(unary_q.astype(jnp.float32) / 32.0)
    pair_factor = jnp.exp(potential_q.astype(jnp.float32) / 64.0)
    pair_table = pair_factor.astype(jnp.bfloat16)
    unit_field = jnp.ones(unary_factor.shape, jnp.bfloat16)
    incoming = [unit_field] * 6
    history = [incoming]
    for iteration in range(ITERS):
        product = cell_product(unary_factor, incoming)
        arriving = []
        for direction in range(6):
            cavity = (product / incoming[OPPOSITE[direction]].astype(jnp.float32)).astype(jnp.bfloat16)
            scores = project(cavity, pair_table)
            totals = lax.optimization_barrier(jnp.sum(scores, axis=-1, keepdims=True))
            message = (L * scores / totals).astype(jnp.bfloat16)
            arriving.append(shift_in(message, direction // 2, direction % 2 == 0, 1.0))
        incoming = arriving
        history.append(incoming)
    product = cell_product(unary_factor, incoming)
    belief = product / lax.optimization_barrier(jnp.sum(product, axis=-1, keepdims=True))
    target = belief_grad.astype(jnp.float32)
    unary_grad = target - belief * lax.optimization_barrier(jnp.sum(target, axis=-1, keepdims=True))
    gradients = [(unary_grad / incoming[direction].astype(jnp.float32)).astype(jnp.bfloat16) for direction in range(6)]
    pair_grad = jnp.zeros((L, L), jnp.float32)
    for iteration in range(ITERS, 0, -1):
        before = history[iteration - 1]
        product = cell_product(unary_factor, before)
        product_grad = jnp.zeros_like(product)
        lifted = []
        for direction in range(6):
            back_grad = shift_back(gradients[direction], direction // 2, direction % 2 == 0).astype(jnp.float32)
            cavity = (product / before[OPPOSITE[direction]].astype(jnp.float32)).astype(jnp.bfloat16)
            scores = project(cavity, pair_table)
            totals = lax.optimization_barrier(jnp.sum(scores, axis=-1, keepdims=True))
            weight = lax.optimization_barrier(jnp.sum(back_grad * scores, axis=-1, keepdims=True)) / totals
            score_grad = (L / totals * (back_grad - weight)).astype(jnp.bfloat16)
            cavity_grad = project(score_grad, pair_table.T)
            pair_grad = pair_grad + jnp.dot(cavity.reshape(-1, L).T, score_grad.reshape(-1, L), preferred_element_type=jnp.float32)
            product_grad = product_grad + cavity_grad / before[OPPOSITE[direction]].astype(jnp.float32)
            lifted.append(cavity_grad)
        unary_grad = unary_grad + product_grad * product
        if iteration > 1:
            gradients = [(product / before[direction].astype(jnp.float32) * (product_grad - lifted[OPPOSITE[direction]] / before[direction].astype(jnp.float32))).astype(jnp.bfloat16) for direction in range(6)]
    potential_grad = pair_factor * pair_grad * (L / math.sqrt(CELLS))
    return (unary_grad, potential_grad)
```

```python
import math

import jax
import jax.numpy as jnp
from jax import lax
from jax.experimental import pallas as pl
from jax.experimental.pallas import tpu as pltpu
from jax.sharding import PartitionSpec as P

LABELS = 128
CELLS = 131072
AXES = ("gx", "gy", "gz")
F32 = jnp.float32
BF16 = jnp.bfloat16
MESH = pl.DeviceIdType.MESH


def take(ref, lead, axis, upper):
    if axis == 0:
        return ref[(*lead, 8 if upper else 1)]
    if axis == 1:
        rows = pl.ds(56 if upper else 0, 8)
    else:
        rows = pl.ds(7 if upper else 0, 8, stride=8)
    return ref[(*lead, pl.ds(1, 8), rows)].reshape(64, LABELS)


def put(ref, lead, axis, upper, value):
    if axis == 0:
        ref[(*lead, 8 if upper else 1)] = value
        return
    if axis == 1:
        rows = pl.ds(56 if upper else 0, 8)
    else:
        rows = pl.ds(7 if upper else 0, 8, stride=8)
    ref[(*lead, pl.ds(1, 8), rows)] = value.reshape(8, 8, LABELS)


def turn(value, steps):
    rows = value.shape[0]
    tiles = value.reshape(rows // 8, 8, LABELS)
    return pltpu.roll(tiles, steps % 8, 1).reshape(rows, LABELS)


def dot(a, b):
    return jnp.dot(a.astype(BF16), b, preferred_element_type=F32)


def dot_rows(a, b):
    return lax.dot_general(a, b, (((0,), (0,)), ((), ())), preferred_element_type=F32)


def lanes(value):
    return jnp.sum(value, axis=-1, keepdims=True)


def wide(value):
    return jnp.broadcast_to(value, (value.shape[0], LABELS))


def cavities(unary, incoming):
    xs = incoming[0] * incoming[1]
    ys = incoming[2] * incoming[3]
    zs = incoming[4] * incoming[5]
    ux = unary * xs
    no_z = ux * ys
    no_y = ux * zs
    no_x = unary * ys * zs
    rest = (no_x, no_x, no_y, no_y, no_z, no_z)
    return [rest[d] * incoming[d] for d in range(6)], no_z * zs


def kernel(
    q_hbm, pot_hbm, bg_hbm, ug_hbm, pg_hbm,
    q, pot, bg, table, table_t, unary, inc, cav, cav16, inv_s, inv_t, inv_s1, inv_t1,
    log_grad, parts, whole, sgrad16, pair, ug, out_face, in_face, ghost_u, ghost_is, ghost_it,
    part1, part2, sum16, sums, final,
    in_sem, out_sem, face_ss, face_rs, s1_ss, s1_rs, s2_ss, s2_rs, s3_ss, s3_rs,
):
    gx, gy, gz = (lax.axis_index(a) for a in AXES)
    nx, ny, nz = (lax.axis_size(a) for a in AXES)

    def beside(axis, step):
        at = [gx, gy, gz]
        size = (nx, ny, nz)[axis]
        at[axis] = lax.rem(at[axis] + step + size, size)
        return tuple(at)

    neighbour = [beside(d // 2, 1 - 2 * (d % 2)) for d in range(6)]
    at_low = (gx == 0, gy == 0, gz == 0)
    at_high = (gx == nx - 1, gy == ny - 1, gz == nz - 1)
    outside = [(at_high if d % 2 else at_low)[d // 2] for d in range(6)]

    core = lax.rem(gz, 2)
    first_id = gx * 2 + core
    firsts = nx * 2
    second_id = gy * (nz // 2) + gz // 2
    seconds = ny * (nz // 2)

    def first_peer(k):
        j = lax.rem(first_id + k, firsts)
        return (j // 2, gy, gz - core + lax.rem(j, 2))

    def second_peer(k):
        j = lax.rem(second_id + k, seconds)
        return (gx, j // (nz // 2), lax.rem(j, nz // 2) * 2 + core)

    loads = [
        pltpu.make_async_copy(q_hbm, q, in_sem.at[0]),
        pltpu.make_async_copy(pot_hbm, pot, in_sem.at[1]),
        pltpu.make_async_copy(bg_hbm, bg, in_sem.at[2]),
    ]
    for load in loads:
        load.start()
    barrier = pltpu.get_barrier_semaphore()
    met = 0
    for place in neighbour:
        pl.semaphore_signal(barrier, inc=1, device_id=place, device_id_type=MESH)
        met += 1
    for k in range(1, firsts):
        pl.semaphore_signal(barrier, inc=1, device_id=first_peer(k), device_id_type=MESH)
        met += 1
    for k in range(1, seconds):
        pl.semaphore_signal(barrier, inc=1, device_id=second_peer(k), device_id_type=MESH)
        met += 1

    started = []

    def send(stage, slot, target, value):
        out_face[stage, slot] = value.astype(BF16)
        copy = pltpu.make_async_remote_copy(
            src_ref=out_face.at[stage, slot],
            dst_ref=in_face.at[stage, slot],
            send_sem=face_ss.at[stage, slot],
            recv_sem=face_rs.at[stage, slot],
            device_id=target,
            device_id_type=MESH,
        )
        copy.start()
        started.append(copy)
        return copy

    loads[0].wait()

    def factors(x, _):
        unary[x + 1] = q[x].astype(F32)
        return 0

    lax.fori_loop(0, 8, factors, 0)
    pl.semaphore_wait(barrier, met)
    copies = [send(0, d, neighbour[d], take(unary, (), d // 2, d % 2 == 0)) for d in range(6)]

    loads[1].wait()
    factor = jnp.exp(pot[...].astype(F32) / 64.0)
    table[...] = factor.astype(BF16)
    table_t[...] = factor.T.astype(BF16)

    def push(t, d, x, message):
        if d == 0:
            inc[t, d, x + 2] = message
        elif d == 1:
            inc[t, d, x] = message
        elif d == 2:
            inc[t, d, x + 1, pl.ds(8, 56)] = message[:56]
        elif d == 3:
            inc[t, d, x + 1, pl.ds(0, 56)] = message[8:]
        elif d == 4:
            inc[t, d, x + 1] = turn(message, 1)
        else:
            inc[t, d, x + 1] = turn(message, -1)

    def first_messages(x, _):
        value = jnp.exp(unary[x + 1] / 32.0)
        unary[x + 1] = value
        scores = dot(value, table[...])
        inv_total = 1.0 / lanes(scores)
        inv_s1[x + 1] = 1.0 / scores
        inv_t1[x + 1] = wide(inv_total)
        message = scores * (LABELS * inv_total)
        for d in range(6):
            push(0, d, x, message)
        return 0

    lax.fori_loop(0, 8, first_messages, 0)

    for copy in copies:
        copy.wait_recv()
    value = jnp.exp(in_face[0].astype(F32).reshape(384, LABELS) / 32.0)
    scores = dot(value, table[...])
    inv_total = 1.0 / lanes(scores)
    ghost_u[...] = value.astype(BF16)
    ghost_is[...] = 1.0 / scores
    ghost_it[...] = wide(inv_total)
    message = scores * (LABELS * inv_total)
    for d in range(6):
        face = message[d * 64 : d * 64 + 64]
        put(inc, (0, d), d // 2, d % 2 == 1, jnp.where(outside[d], 1.0, face))

    for t in (1, 2):
        faces = []
        for d in range(6):
            value = take(unary, (), d // 2, d % 2 == 0)
            for e in range(6):
                if e != d ^ 1:
                    value = value * take(inc, (t - 1, e), d // 2, d % 2 == 0)
            faces.append(value.astype(BF16))
        scores = dot(jnp.concatenate(faces, axis=0), table[...])
        message = scores * (LABELS / lanes(scores))
        copies = [send(t, d, neighbour[d], message[d * 64 : d * 64 + 64]) for d in range(6)]

        def messages(x, _, t=t):
            values, _ = cavities(unary[x + 1], [inc[t - 1, d, x + 1] for d in range(6)])
            for d in range(6):
                rounded = values[d].astype(BF16)
                cav[t - 1, d, x + 1] = values[d]
                cav16[t - 1, d, x] = rounded
                scores = dot(rounded, table[...])
                inv_total = 1.0 / lanes(scores)
                inv_s[t - 1, d, x + 1] = 1.0 / scores
                inv_t[t - 1, d, x + 1] = wide(inv_total)
                push(t, d, x, scores * (LABELS * inv_total))
            return 0

        lax.fori_loop(0, 8, messages, 0)
        for copy in copies:
            copy.wait_recv()
        for d in range(6):
            face = in_face[t, d].astype(F32)
            put(inc, (t, d), d // 2, d % 2 == 1, jnp.where(outside[d], 1.0, face))

    loads[2].wait()
    empty = jnp.zeros((64, LABELS), F32)
    for x in (0, 9):
        log_grad[x] = empty
        for t in range(2):
            whole[t, x] = empty
            for d in range(6):
                parts[t, d, x] = empty

    def beliefs(x, _):
        product = unary[x + 1]
        for d in range(6):
            product = product * inc[2, d, x + 1]
        target = bg[x].astype(F32)
        log_grad[x + 1] = target - product * (lanes(target) / lanes(product))
        return 0

    lax.fori_loop(0, 8, beliefs, 0)
    copies = [send(3, d, neighbour[d ^ 1], take(log_grad, (), d // 2, d % 2 == 1)) for d in range(6)]

    place = lax.rem(lax.broadcasted_iota(jnp.int32, (64, LABELS), 0), 8)
    border = jnp.zeros((8, LABELS), F32)

    def arrived(read, d, x):
        if d == 0:
            return read(d, x + 2)
        if d == 1:
            return read(d, x)
        if d == 2:
            return jnp.concatenate([read(d, x + 1)[8:], border], axis=0)
        if d == 3:
            return jnp.concatenate([border, read(d, x + 1)[:56]], axis=0)
        if d == 4:
            return jnp.where(place == 7, 0.0, turn(read(d, x + 1), -1))
        return jnp.where(place == 0, 0.0, turn(read(d, x + 1), 1))

    def last_grads(d, x):
        return log_grad[x]

    def grads_of(t):
        return lambda d, x: whole[t, x] - parts[t, d ^ 1, x]

    pair[...] = jnp.zeros_like(pair)

    for t in (1, 0):
        read = last_grads if t == 1 else grads_of(1)

        def backward(x, _, t=t, read=read):
            total = None
            for d in range(6):
                grad = arrived(read, d, x)
                score_grad = grad * inv_s[t, d, x + 1] - lanes(grad) * inv_t[t, d, x + 1]
                rounded = score_grad.astype(BF16)
                sgrad16[d, x] = rounded
                part = dot(rounded, table_t[...]) * cav[t, d, x + 1]
                parts[t, d, x + 1] = part
                total = part if total is None else total + part
            whole[t, x + 1] = total
            return 0

        lax.fori_loop(0, 8, backward, 0)

        def pair_terms(d, _, t=t):
            pair[...] += dot_rows(
                cav16[t, d].reshape(512, LABELS), sgrad16[d].reshape(512, LABELS)
            )
            return 0

        lax.fori_loop(0, 6, pair_terms, 0)
        for copy in copies:
            copy.wait_recv()
        rounded, factors_at = [], []
        for d in range(6):
            upper = d % 2 == 0
            grad = jnp.where(outside[d ^ 1], 0.0, in_face[4 - t, d].astype(F32))
            score_grad = grad * take(inv_s, (t, d), d // 2, upper)
            score_grad -= lanes(grad) * take(inv_t, (t, d), d // 2, upper)
            rounded.append(score_grad.astype(BF16))
            factors_at.append(take(cav, (t, d), d // 2, upper))
        rounded = jnp.concatenate(rounded, axis=0)
        back = dot(rounded, table_t[...])
        for d in range(6):
            upper = d % 2 == 0
            part = back[d * 64 : d * 64 + 64] * factors_at[d]
            put(parts, (t, d), d // 2, upper, part)
            put(whole, (t,), d // 2, upper, take(whole, (t,), d // 2, upper) + part)
        copies = []
        edge = []
        for d in range(6):
            upper = d % 2 == 1
            grad = take(whole, (t,), d // 2, upper) - take(parts, (t, d ^ 1), d // 2, upper)
            copies.append(send(5 - t, d, neighbour[d ^ 1], grad))
            edge.append(grad)
        at = jnp.concatenate(factors_at, axis=0).astype(BF16)
        pair[...] += dot_rows(at, rounded)

    read = grads_of(0)

    def first_grads(x, _):
        grad = arrived(read, 0, x)
        for d in range(1, 6):
            grad += arrived(read, d, x)
        log_sum = grad * inv_s1[x + 1] - lanes(grad) * inv_t1[x + 1]
        rounded = log_sum.astype(BF16)
        sgrad16[0, x] = rounded
        back = dot(rounded, table_t[...]) * unary[x + 1]
        ug[x + 1] = log_grad[x + 1] + whole[1, x + 1] + whole[0, x + 1] + back
        cav16[0, 0, x] = unary[x + 1].astype(BF16)
        return 0

    lax.fori_loop(0, 8, first_grads, 0)
    pair[...] += dot_rows(cav16[0, 0].reshape(512, LABELS), sgrad16[0].reshape(512, LABELS))
    grad = jnp.concatenate([jnp.where(outside[d], 0.0, edge[d]) for d in range(6)], axis=0)
    score_grad = grad * ghost_is[...] - lanes(grad) * ghost_it[...]
    pair[...] += dot_rows(ghost_u[...], score_grad.astype(BF16))

    def copy_to(src, dst, ss, rs, target):
        copy = pltpu.make_async_remote_copy(
            src_ref=src, dst_ref=dst, send_sem=ss, recv_sem=rs, device_id=target, device_id_type=MESH
        )
        copy.start()
        started.append(copy)
        return copy

    height = LABELS // firsts

    def rows_of(j):
        return pl.ds(pl.multiple_of(j * height, height), height)

    sends = [
        copy_to(
            pair.at[rows_of(lax.rem(first_id + k, firsts))], part1.at[k - 1],
            s1_ss.at[k - 1], s1_rs.at[k - 1], first_peer(k),
        )
        for k in range(1, firsts)
    ]

    for copy in copies:
        copy.wait_recv()
    rounded = []
    for d in range(6):
        upper = d % 2 == 0
        grad = jnp.where(outside[d ^ 1], 0.0, in_face[5, d].astype(F32))
        score_grad = grad * take(inv_s1, (), d // 2, upper)
        score_grad -= lanes(grad) * take(inv_t1, (), d // 2, upper)
        rounded.append(score_grad.astype(BF16))
    back = dot(jnp.concatenate(rounded, axis=0), table_t[...])
    for d in range(6):
        upper = d % 2 == 0
        part = back[d * 64 : d * 64 + 64] * take(unary, (), d // 2, upper)
        put(ug, (), d // 2, upper, take(ug, (), d // 2, upper) + part)
    store = pltpu.make_async_copy(ug.at[pl.ds(1, 8)], ug_hbm, out_sem.at[0])
    store.start()

    for copy in sends:
        copy.wait_recv()
    mine = pair[rows_of(first_id)]
    for k in range(1, firsts):
        mine += part1[k - 1]
    sums[...] = mine
    sum16[...] = mine.astype(BF16)
    sends = [
        copy_to(sum16, part2.at[k - 1], s2_ss.at[k - 1], s2_rs.at[k - 1], second_peer(k))
        for k in range(1, seconds)
    ]
    for copy in sends:
        copy.wait_recv()
    mine = sums[...]
    for k in range(1, seconds):
        mine += part2[k - 1].astype(F32)
    final[rows_of(first_id)] = mine
    here = final.at[rows_of(first_id)]
    sends = [
        copy_to(here, here, s3_ss.at[k - 1], s3_rs.at[k - 1], first_peer(k))
        for k in range(1, firsts)
    ]
    for copy in sends:
        copy.wait_recv()
    factor = jnp.exp(pot[...].astype(F32) / 64.0)
    for copy in started:
        copy.wait_send()
    pair[...] = factor * final[...] * (LABELS / math.sqrt(CELLS))
    store2 = pltpu.make_async_copy(pair, pg_hbm, out_sem.at[1])
    store2.start()
    store.wait()
    store2.wait()


def on_device(unary_q, potential_q, belief_grad):
    slabs = (8, 64, LABELS)
    padded = (10, 64, LABELS)
    firsts = lax.axis_size("gx") * 2
    seconds = lax.axis_size("gy") * (lax.axis_size("gz") // 2)
    height = LABELS // firsts
    vmem, dma = pltpu.VMEM, pltpu.SemaphoreType.DMA
    any_space = pl.BlockSpec(memory_space=pl.ANY)
    unary_grad, potential_grad = pl.pallas_call(
        kernel,
        out_shape=(
            jax.ShapeDtypeStruct(slabs, F32),
            jax.ShapeDtypeStruct((LABELS, LABELS), F32),
        ),
        in_specs=[any_space] * 3,
        out_specs=(any_space, any_space),
        scratch_shapes=[
            vmem(slabs, jnp.int32),
            vmem((LABELS, LABELS), jnp.int32),
            vmem(slabs, BF16),
            vmem((LABELS, LABELS), BF16),
            vmem((LABELS, LABELS), BF16),
            vmem(padded, F32),
            vmem((3, 6, *padded), F32),
            vmem((2, 6, *padded), F32),
            vmem((2, 6, *slabs), BF16),
            vmem((2, 6, *padded), F32),
            vmem((2, 6, *padded), F32),
            vmem(padded, F32),
            vmem(padded, F32),
            vmem(padded, F32),
            vmem((2, 6, *padded), F32),
            vmem((2, *padded), F32),
            vmem((6, *slabs), BF16),
            vmem((LABELS, LABELS), F32),
            vmem(padded, F32),
            vmem((6, 6, 64, LABELS), BF16),
            vmem((6, 6, 64, LABELS), BF16),
            vmem((384, LABELS), BF16),
            vmem((384, LABELS), F32),
            vmem((384, LABELS), F32),
            vmem((firsts - 1, height, LABELS), F32),
            vmem((seconds - 1, height, LABELS), BF16),
            vmem((height, LABELS), BF16),
            vmem((height, LABELS), F32),
            vmem((LABELS, LABELS), F32),
            dma((3,)),
            dma((2,)),
            dma((6, 6)),
            dma((6, 6)),
            dma((firsts - 1,)),
            dma((firsts - 1,)),
            dma((seconds - 1,)),
            dma((seconds - 1,)),
            dma((firsts - 1,)),
            dma((firsts - 1,)),
        ],
        compiler_params=pltpu.CompilerParams(
            collective_id=0, has_side_effects=True, vmem_limit_bytes=48 * 2**20
        ),
    )(unary_q.reshape(slabs), potential_q, belief_grad.reshape(slabs))
    return unary_grad.reshape(unary_q.shape), potential_grad


def solution(mesh):
    return jax.shard_map(
        on_device,
        mesh=mesh,
        in_specs=(P("gx", "gy", "gz", None), P(), P("gx", "gy", "gz", None)),
        out_specs=(P("gx", "gy", "gz", None), P()),
        check_vma=False,
    )
```

```python
import math

import jax
import jax.numpy as jnp
from jax import lax
from jax.experimental import pallas as pl
from jax.experimental.pallas import tpu as pltpu
from jax.sharding import PartitionSpec as P

LABELS = 128
CELLS = 131072
AXES = ("gx", "gy", "gz")
F32 = jnp.float32
BF16 = jnp.bfloat16
MESH = pl.DeviceIdType.MESH


def take(ref, lead, axis, upper):
    if axis == 0:
        return ref[(*lead, 8 if upper else 1)]
    if axis == 1:
        rows = pl.ds(56 if upper else 0, 8)
    else:
        rows = pl.ds(7 if upper else 0, 8, stride=8)
    return ref[(*lead, pl.ds(1, 8), rows)].reshape(64, LABELS)


def put(ref, lead, axis, upper, value):
    if axis == 0:
        ref[(*lead, 8 if upper else 1)] = value
        return
    if axis == 1:
        rows = pl.ds(56 if upper else 0, 8)
    else:
        rows = pl.ds(7 if upper else 0, 8, stride=8)
    ref[(*lead, pl.ds(1, 8), rows)] = value.reshape(8, 8, LABELS)


def turn(value, steps):
    rows = value.shape[0]
    tiles = value.reshape(rows // 8, 8, LABELS)
    return pltpu.roll(tiles, steps % 8, 1).reshape(rows, LABELS)


def dot(a, b):
    return jnp.dot(a.astype(BF16), b, preferred_element_type=F32)


def dot_rows(a, b):
    return lax.dot_general(a, b, (((0,), (0,)), ((), ())), preferred_element_type=F32)


def lanes(value):
    return jnp.sum(value, axis=-1, keepdims=True)


def wide(value):
    return jnp.broadcast_to(value, (value.shape[0], LABELS))


def cavities(unary, incoming):
    xs = incoming[0] * incoming[1]
    ys = incoming[2] * incoming[3]
    zs = incoming[4] * incoming[5]
    ux = unary * xs
    no_z = ux * ys
    no_y = ux * zs
    no_x = unary * ys * zs
    rest = (no_x, no_x, no_y, no_y, no_z, no_z)
    return [rest[d] * incoming[d] for d in range(6)], no_z * zs


def kernel(
    q_hbm, pot_hbm, bg_hbm, ug_out, pg_out,
    q, pot, bg, table, table_t, unary, inc, cav, cav16, inv_s, inv_t, inv_s1, inv_t1,
    log_grad, parts, whole, sgrad16, pair, ug, out_face, in_face, ghost_u, ghost_is, ghost_it,
    part1, part2, final,
    in_sem, out_sem, face_ss, face_rs, s1_ss, s1_rs, s2_ss, s2_rs, s3_ss, s3_rs,
):
    gx, gy, gz = (lax.axis_index(a) for a in AXES)
    nx, ny, nz = (lax.axis_size(a) for a in AXES)

    def beside(axis, step):
        at = [gx, gy, gz]
        size = (nx, ny, nz)[axis]
        at[axis] = lax.rem(at[axis] + step + size, size)
        return tuple(at)

    neighbour = [beside(d // 2, 1 - 2 * (d % 2)) for d in range(6)]
    at_low = (gx == 0, gy == 0, gz == 0)
    at_high = (gx == nx - 1, gy == ny - 1, gz == nz - 1)
    outside = [(at_high if d % 2 else at_low)[d // 2] for d in range(6)]

    core = lax.rem(gz, 2)
    first_id = gx * 2 + core
    firsts = nx * 2
    second_id = gy * (nz // 2) + gz // 2
    seconds = ny * (nz // 2)

    def first_peer(k):
        j = lax.rem(first_id + k, firsts)
        return (j // 2, gy, gz - core + lax.rem(j, 2))

    def second_peer(k):
        j = lax.rem(second_id + k, seconds)
        return (gx, j // (nz // 2), lax.rem(j, nz // 2) * 2 + core)

    loads = [
        pltpu.make_async_copy(q_hbm, q, in_sem.at[0]),
        pltpu.make_async_copy(pot_hbm, pot, in_sem.at[1]),
        pltpu.make_async_copy(bg_hbm, bg, in_sem.at[2]),
    ]
    for load in loads:
        load.start()
    barrier = pltpu.get_barrier_semaphore()
    met = 0
    for place in neighbour:
        pl.semaphore_signal(barrier, inc=1, device_id=place, device_id_type=MESH)
        met += 1
    for k in range(1, firsts):
        pl.semaphore_signal(barrier, inc=1, device_id=first_peer(k), device_id_type=MESH)
        met += 1
    for k in range(1, seconds):
        pl.semaphore_signal(barrier, inc=1, device_id=second_peer(k), device_id_type=MESH)
        met += 1

    started = []

    def send(stage, slot, target, value):
        out_face[stage, slot] = value.astype(BF16)
        copy = pltpu.make_async_remote_copy(
            src_ref=out_face.at[stage, slot],
            dst_ref=in_face.at[stage, slot],
            send_sem=face_ss.at[stage, slot],
            recv_sem=face_rs.at[stage, slot],
            device_id=target,
            device_id_type=MESH,
        )
        copy.start()
        started.append(copy)
        return copy

    loads[0].wait()

    def factors(x, _):
        unary[x + 1] = q[x].astype(F32)
        return 0

    lax.fori_loop(0, 8, factors, 0, unroll=True)
    pl.semaphore_wait(barrier, met)
    copies = [send(0, d, neighbour[d], take(unary, (), d // 2, d % 2 == 0)) for d in range(6)]

    loads[1].wait()
    factor = jnp.exp(pot[...].astype(F32) / 64.0)
    table[...] = factor.astype(BF16)
    table_t[...] = factor.T.astype(BF16)

    def push(t, d, x, message):
        if d == 0:
            inc[t, d, x + 2] = message
        elif d == 1:
            inc[t, d, x] = message
        elif d == 2:
            inc[t, d, x + 1, pl.ds(8, 56)] = message[:56]
        elif d == 3:
            inc[t, d, x + 1, pl.ds(0, 56)] = message[8:]
        elif d == 4:
            inc[t, d, x + 1] = turn(message, 1)
        else:
            inc[t, d, x + 1] = turn(message, -1)

    def first_messages(x, _):
        value = jnp.exp(unary[x + 1] / 32.0)
        unary[x + 1] = value
        scores = dot(value, table[...])
        inv_total = 1.0 / lanes(scores)
        inv_s1[x + 1] = 1.0 / scores
        inv_t1[x + 1] = wide(inv_total)
        message = scores * (LABELS * inv_total)
        for d in range(6):
            push(0, d, x, message)
        return 0

    lax.fori_loop(0, 8, first_messages, 0, unroll=True)

    for copy in copies:
        copy.wait_recv()
    value = jnp.exp(in_face[0].astype(F32).reshape(384, LABELS) / 32.0)
    scores = dot(value, table[...])
    inv_total = 1.0 / lanes(scores)
    ghost_u[...] = value.astype(BF16)
    ghost_is[...] = 1.0 / scores
    ghost_it[...] = wide(inv_total)
    message = scores * (LABELS * inv_total)
    for d in range(6):
        face = message[d * 64 : d * 64 + 64]
        put(inc, (0, d), d // 2, d % 2 == 1, jnp.where(outside[d], 1.0, face))

    for t in (1, 2):
        faces = []
        for d in range(6):
            value = take(unary, (), d // 2, d % 2 == 0)
            for e in range(6):
                if e != d ^ 1:
                    value = value * take(inc, (t - 1, e), d // 2, d % 2 == 0)
            faces.append(value.astype(BF16))
        scores = dot(jnp.concatenate(faces, axis=0), table[...])
        message = scores * (LABELS / lanes(scores))
        copies = [send(t, d, neighbour[d], message[d * 64 : d * 64 + 64]) for d in range(6)]

        def messages(x, _, t=t):
            values, _ = cavities(unary[x + 1], [inc[t - 1, d, x + 1] for d in range(6)])
            for d in range(6):
                rounded = values[d].astype(BF16)
                cav[t - 1, d, x + 1] = values[d]
                cav16[t - 1, d, x] = rounded
                scores = dot(rounded, table[...])
                inv_total = 1.0 / lanes(scores)
                inv_s[t - 1, d, x + 1] = 1.0 / scores
                inv_t[t - 1, d, x + 1] = wide(inv_total)
                push(t, d, x, scores * (LABELS * inv_total))
            return 0

        lax.fori_loop(0, 8, messages, 0, unroll=True)
        for copy in copies:
            copy.wait_recv()
        for d in range(6):
            face = in_face[t, d].astype(F32)
            put(inc, (t, d), d // 2, d % 2 == 1, jnp.where(outside[d], 1.0, face))

    loads[2].wait()
    empty = jnp.zeros((64, LABELS), F32)
    for x in (0, 9):
        log_grad[x] = empty
        for t in range(2):
            whole[t, x] = empty
            for d in range(6):
                parts[t, d, x] = empty

    def beliefs(x, _):
        product = unary[x + 1]
        for d in range(6):
            product = product * inc[2, d, x + 1]
        target = bg[x].astype(F32)
        log_grad[x + 1] = target - product * (lanes(target) / lanes(product))
        return 0

    lax.fori_loop(0, 8, beliefs, 0, unroll=True)
    copies = [send(3, d, neighbour[d ^ 1], take(log_grad, (), d // 2, d % 2 == 1)) for d in range(6)]

    place = lax.rem(lax.broadcasted_iota(jnp.int32, (64, LABELS), 0), 8)
    border = jnp.zeros((8, LABELS), F32)

    def arrived(read, d, x):
        if d == 0:
            return read(d, x + 2)
        if d == 1:
            return read(d, x)
        if d == 2:
            return jnp.concatenate([read(d, x + 1)[8:], border], axis=0)
        if d == 3:
            return jnp.concatenate([border, read(d, x + 1)[:56]], axis=0)
        if d == 4:
            return jnp.where(place == 7, 0.0, turn(read(d, x + 1), -1))
        return jnp.where(place == 0, 0.0, turn(read(d, x + 1), 1))

    def last_grads(d, x):
        return log_grad[x]

    def grads_of(t):
        return lambda d, x: whole[t, x] - parts[t, d ^ 1, x]

    pair[...] = jnp.zeros_like(pair)

    for t in (1, 0):
        read = last_grads if t == 1 else grads_of(1)

        def backward(x, _, t=t, read=read):
            total = None
            for d in range(6):
                grad = arrived(read, d, x)
                score_grad = grad * inv_s[t, d, x + 1] - lanes(grad) * inv_t[t, d, x + 1]
                rounded = score_grad.astype(BF16)
                sgrad16[d, x] = rounded
                part = dot(rounded, table_t[...]) * cav[t, d, x + 1]
                parts[t, d, x + 1] = part
                total = part if total is None else total + part
            whole[t, x + 1] = total
            return 0

        lax.fori_loop(0, 8, backward, 0, unroll=True)

        def pair_terms(d, _, t=t):
            pair[...] += dot_rows(
                cav16[t, d].reshape(512, LABELS), sgrad16[d].reshape(512, LABELS)
            )
            return 0

        lax.fori_loop(0, 6, pair_terms, 0, unroll=True)
        for copy in copies:
            copy.wait_recv()
        rounded, factors_at = [], []
        for d in range(6):
            upper = d % 2 == 0
            grad = jnp.where(outside[d ^ 1], 0.0, in_face[4 - t, d].astype(F32))
            score_grad = grad * take(inv_s, (t, d), d // 2, upper)
            score_grad -= lanes(grad) * take(inv_t, (t, d), d // 2, upper)
            rounded.append(score_grad.astype(BF16))
            factors_at.append(take(cav, (t, d), d // 2, upper))
        rounded = jnp.concatenate(rounded, axis=0)
        back = dot(rounded, table_t[...])
        for d in range(6):
            upper = d % 2 == 0
            part = back[d * 64 : d * 64 + 64] * factors_at[d]
            put(parts, (t, d), d // 2, upper, part)
            put(whole, (t,), d // 2, upper, take(whole, (t,), d // 2, upper) + part)
        copies = []
        edge = []
        for d in range(6):
            upper = d % 2 == 1
            grad = take(whole, (t,), d // 2, upper) - take(parts, (t, d ^ 1), d // 2, upper)
            copies.append(send(5 - t, d, neighbour[d ^ 1], grad))
            edge.append(grad)
        at = jnp.concatenate(factors_at, axis=0).astype(BF16)
        pair[...] += dot_rows(at, rounded)

    read = grads_of(0)

    def first_grads(x, _):
        grad = arrived(read, 0, x)
        for d in range(1, 6):
            grad += arrived(read, d, x)
        log_sum = grad * inv_s1[x + 1] - lanes(grad) * inv_t1[x + 1]
        rounded = log_sum.astype(BF16)
        sgrad16[0, x] = rounded
        back = dot(rounded, table_t[...]) * unary[x + 1]
        ug[x + 1] = log_grad[x + 1] + whole[1, x + 1] + whole[0, x + 1] + back
        cav16[0, 0, x] = unary[x + 1].astype(BF16)
        return 0

    lax.fori_loop(0, 8, first_grads, 0, unroll=True)
    pair[...] += dot_rows(cav16[0, 0].reshape(512, LABELS), sgrad16[0].reshape(512, LABELS))
    grad = jnp.concatenate([jnp.where(outside[d], 0.0, edge[d]) for d in range(6)], axis=0)
    score_grad = grad * ghost_is[...] - lanes(grad) * ghost_it[...]
    pair[...] += dot_rows(ghost_u[...], score_grad.astype(BF16))

    def copy_to(src, dst, ss, rs, target):
        copy = pltpu.make_async_remote_copy(
            src_ref=src, dst_ref=dst, send_sem=ss, recv_sem=rs, device_id=target, device_id_type=MESH
        )
        copy.start()
        started.append(copy)
        return copy

    height = LABELS // firsts

    def rows_of(j):
        return pl.ds(pl.multiple_of(j * height, height), height)

    sends = [
        copy_to(
            pair.at[rows_of(lax.rem(first_id + k, firsts))], part1.at[k - 1],
            s1_ss.at[k - 1], s1_rs.at[k - 1], first_peer(k),
        )
        for k in range(1, firsts)
    ]

    for copy in copies:
        copy.wait_recv()
    rounded = []
    for d in range(6):
        upper = d % 2 == 0
        grad = jnp.where(outside[d ^ 1], 0.0, in_face[5, d].astype(F32))
        score_grad = grad * take(inv_s1, (), d // 2, upper)
        score_grad -= lanes(grad) * take(inv_t1, (), d // 2, upper)
        rounded.append(score_grad.astype(BF16))
    back = dot(jnp.concatenate(rounded, axis=0), table_t[...])
    for d in range(6):
        upper = d % 2 == 0
        part = back[d * 64 : d * 64 + 64] * take(unary, (), d // 2, upper)
        put(ug, (), d // 2, upper, take(ug, (), d // 2, upper) + part)
    store = pltpu.make_async_copy(ug.at[pl.ds(1, 8)], ug_out, out_sem.at[0])
    store.start()

    for copy in sends:
        copy.wait_recv()
    mine = pair[rows_of(first_id)]
    for k in range(1, firsts):
        mine += part1[k - 1]
    part2[second_id] = mine.astype(BF16)
    own = part2.at[second_id]
    sends = [
        copy_to(own, own, s2_ss.at[k - 1], s2_rs.at[k - 1], second_peer(k))
        for k in range(1, seconds)
    ]
    for copy in sends:
        copy.wait_recv()
    final[rows_of(first_id)] = jnp.sum(part2[...].astype(F32), axis=0)
    here = final.at[rows_of(first_id)]
    sends = [
        copy_to(here, here, s3_ss.at[k - 1], s3_rs.at[k - 1], first_peer(k))
        for k in range(1, firsts)
    ]
    for copy in sends:
        copy.wait_recv()
    factor = jnp.exp(pot[...].astype(F32) / 64.0)
    for copy in started:
        copy.wait_send()
    pair[...] = factor * final[...] * (LABELS / math.sqrt(CELLS))
    store2 = pltpu.make_async_copy(pair, pg_out, out_sem.at[1])
    store2.start()
    store.wait()
    store2.wait()


def on_device(unary_q, potential_q, belief_grad):
    slabs = (8, 64, LABELS)
    padded = (10, 64, LABELS)
    firsts = lax.axis_size("gx") * 2
    seconds = lax.axis_size("gy") * (lax.axis_size("gz") // 2)
    height = LABELS // firsts
    vmem, dma = pltpu.VMEM, pltpu.SemaphoreType.DMA
    unary_grad, potential_grad = pl.pallas_call(
        kernel,
        out_shape=(
            jax.ShapeDtypeStruct(slabs, F32),
            jax.ShapeDtypeStruct((LABELS, LABELS), F32),
        ),
        in_specs=[pl.BlockSpec(memory_space=pltpu.HBM)] * 3,
        out_specs=(pl.BlockSpec(memory_space=pltpu.HBM),) * 2,
        scratch_shapes=[
            vmem(slabs, jnp.int32),
            vmem((LABELS, LABELS), jnp.int32),
            vmem(slabs, BF16),
            vmem((LABELS, LABELS), BF16),
            vmem((LABELS, LABELS), BF16),
            vmem(padded, F32),
            vmem((3, 6, *padded), F32),
            vmem((2, 6, *padded), F32),
            vmem((2, 6, *slabs), BF16),
            vmem((2, 6, *padded), F32),
            vmem((2, 6, *padded), F32),
            vmem(padded, F32),
            vmem(padded, F32),
            vmem(padded, F32),
            vmem((2, 6, *padded), F32),
            vmem((2, *padded), F32),
            vmem((6, *slabs), BF16),
            vmem((LABELS, LABELS), F32),
            vmem(padded, F32),
            vmem((6, 6, 64, LABELS), BF16),
            vmem((6, 6, 64, LABELS), BF16),
            vmem((384, LABELS), BF16),
            vmem((384, LABELS), F32),
            vmem((384, LABELS), F32),
            vmem((firsts - 1, height, LABELS), F32),
            vmem((seconds, height, LABELS), BF16),
            vmem((LABELS, LABELS), F32),
            dma((3,)),
            dma((2,)),
            dma((6, 6)),
            dma((6, 6)),
            dma((firsts - 1,)),
            dma((firsts - 1,)),
            dma((seconds - 1,)),
            dma((seconds - 1,)),
            dma((firsts - 1,)),
            dma((firsts - 1,)),
        ],
        compiler_params=pltpu.CompilerParams(
            collective_id=0, has_side_effects=True, vmem_limit_bytes=60 * 2**20
        ),
    )(unary_q.reshape(slabs), potential_q, belief_grad.reshape(slabs))
    return unary_grad.reshape(unary_q.shape), potential_grad


def solution(mesh):
    return jax.shard_map(
        on_device,
        mesh=mesh,
        in_specs=(P("gx", "gy", "gz", None), P(), P("gx", "gy", "gz", None)),
        out_specs=(P("gx", "gy", "gz", None), P()),
        check_vma=False,
    )
```

```python
import math

import jax
import jax.numpy as jnp
from jax import lax
from jax.experimental import pallas as pl
from jax.experimental.pallas import tpu as pltpu
from jax.sharding import PartitionSpec as P

LABELS = 128
CELLS = 131072
AXES = ("gx", "gy", "gz")
F32 = jnp.float32
BF16 = jnp.bfloat16
MESH = pl.DeviceIdType.MESH
EDGES = [(d, e) for d in range(6) for e in range(d + 1, 6) if d // 2 != e // 2]
GHOSTS = 6 * 128 + len(EDGES) * 8


def take(ref, lead, axis, upper):
    if axis == 0:
        return ref[(*lead, 8 if upper else 1)]
    if axis == 1:
        rows = pl.ds(56 if upper else 0, 8)
    else:
        rows = pl.ds(7 if upper else 0, 8, stride=8)
    return ref[(*lead, pl.ds(1, 8), rows)].reshape(64, LABELS)


def layer(ref, axis, index):
    if axis == 0:
        return ref[index + 1]
    if axis == 1:
        rows = pl.ds(index * 8, 8)
    else:
        rows = pl.ds(index, 8, stride=8)
    return ref[pl.ds(1, 8), rows].reshape(64, LABELS)


def edge_at(d, e):
    return EDGES.index((d, e) if d < e else (e, d))


def put(ref, lead, axis, upper, value):
    if axis == 0:
        ref[(*lead, 8 if upper else 1)] = value
        return
    if axis == 1:
        rows = pl.ds(56 if upper else 0, 8)
    else:
        rows = pl.ds(7 if upper else 0, 8, stride=8)
    ref[(*lead, pl.ds(1, 8), rows)] = value.reshape(8, 8, LABELS)


def turn(value, steps):
    rows = value.shape[0]
    tiles = value.reshape(rows // 8, 8, LABELS)
    return pltpu.roll(tiles, steps % 8, 1).reshape(rows, LABELS)


def dot(a, b):
    return jnp.dot(a.astype(BF16), b, preferred_element_type=F32)


def dot_rows(a, b):
    return lax.dot_general(a, b, (((0,), (0,)), ((), ())), preferred_element_type=F32)


def lanes(value):
    return jnp.sum(value, axis=-1, keepdims=True)


def wide(value):
    return jnp.broadcast_to(value, (value.shape[0], LABELS))


def cavities(unary, incoming):
    xs = incoming[0] * incoming[1]
    ys = incoming[2] * incoming[3]
    zs = incoming[4] * incoming[5]
    ux = unary * xs
    no_z = ux * ys
    no_y = ux * zs
    no_x = unary * ys * zs
    rest = (no_x, no_x, no_y, no_y, no_z, no_z)
    return [rest[d] * incoming[d] for d in range(6)], no_z * zs


def kernel(
    q_hbm, pot_hbm, bg_hbm, ug_out, pg_out,
    q, pot, bg, table, table_t, unary, inc, cav, cav16, inv_s, inv_t, inv_s1, inv_t1,
    log_grad, parts, whole, sgrad16, pair, ug, out_face, in_face, ghost_u, ghost_is, ghost_it, ghost_m, ghost_g,
    ghost_c, ghost_is2, ghost_it2, side, line_out, line_in, halo_out, halo_in,
    part1, part2, final,
    in_sem, out_sem, face_ss, face_rs, halo_ss, halo_rs, line_ss, line_rs, s1_ss, s1_rs, s2_ss, s2_rs, s3_ss, s3_rs,
):
    gx, gy, gz = (lax.axis_index(a) for a in AXES)
    nx, ny, nz = (lax.axis_size(a) for a in AXES)

    def beside(axis, step):
        at = [gx, gy, gz]
        size = (nx, ny, nz)[axis]
        at[axis] = lax.rem(at[axis] + step + size, size)
        return tuple(at)

    neighbour = [beside(d // 2, 1 - 2 * (d % 2)) for d in range(6)]
    across = []
    for d, e in EDGES:
        at = list(neighbour[d])
        at[e // 2] = neighbour[e][e // 2]
        across.append(tuple(at))
    at_low = (gx == 0, gy == 0, gz == 0)
    at_high = (gx == nx - 1, gy == ny - 1, gz == nz - 1)
    outside = [(at_high if d % 2 else at_low)[d // 2] for d in range(6)]

    core = lax.rem(gz, 2)
    first_id = gx * 2 + core
    firsts = nx * 2
    second_id = gy * (nz // 2) + gz // 2
    seconds = ny * (nz // 2)

    def first_peer(k):
        j = lax.rem(first_id + k, firsts)
        return (j // 2, gy, gz - core + lax.rem(j, 2))

    def second_peer(k):
        j = lax.rem(second_id + k, seconds)
        return (gx, j // (nz // 2), lax.rem(j, nz // 2) * 2 + core)

    loads = [
        pltpu.make_async_copy(q_hbm, q, in_sem.at[0]),
        pltpu.make_async_copy(pot_hbm, pot, in_sem.at[1]),
        pltpu.make_async_copy(bg_hbm, bg, in_sem.at[2]),
    ]
    for load in loads:
        load.start()
    barrier = pltpu.get_barrier_semaphore()
    met = 0
    for place in neighbour + across:
        pl.semaphore_signal(barrier, inc=1, device_id=place, device_id_type=MESH)
        met += 1
    for k in range(1, firsts):
        pl.semaphore_signal(barrier, inc=1, device_id=first_peer(k), device_id_type=MESH)
        met += 1
    for k in range(1, seconds):
        pl.semaphore_signal(barrier, inc=1, device_id=second_peer(k), device_id_type=MESH)
        met += 1

    started = []

    def send(stage, slot, target, value):
        out_face[stage, slot] = value.astype(BF16)
        copy = pltpu.make_async_remote_copy(
            src_ref=out_face.at[stage, slot],
            dst_ref=in_face.at[stage, slot],
            send_sem=face_ss.at[stage, slot],
            recv_sem=face_rs.at[stage, slot],
            device_id=target,
            device_id_type=MESH,
        )
        copy.start()
        started.append(copy)
        return copy

    loads[0].wait()

    def factors(x, _):
        unary[x + 1] = q[x].astype(F32)
        return 0

    lax.fori_loop(0, 8, factors, 0, unroll=True)
    pl.semaphore_wait(barrier, met)
    copies = []

    def send_from(src, dst, ss, rs, target):
        copy = pltpu.make_async_remote_copy(
            src_ref=src, dst_ref=dst, send_sem=ss, recv_sem=rs, device_id=target, device_id_type=MESH
        )
        copy.start()
        started.append(copy)
        return copy

    for k, (d, e) in enumerate(EDGES):
        near = [7 if f % 2 == 0 else 0 for f in (d, e)]
        if (d // 2, e // 2) == (0, 1):
            line_out[k] = unary[near[0] + 1, pl.ds(near[1] * 8, 8)]
        elif (d // 2, e // 2) == (0, 2):
            line_out[k] = unary[near[0] + 1, pl.ds(near[1], 8, stride=8)]
        else:
            for x in range(8):
                row = pl.ds(near[0] * 8 + near[1], 1)
                line_out[k, pl.ds(x, 1)] = unary[x + 1, row]
        copies.append(send_from(line_out.at[k], line_in.at[k], line_ss.at[k], line_rs.at[k], across[k]))
    for d in range(6):
        near, behind = (7, 6) if d % 2 == 0 else (0, 1)
        halo_out[d, pl.ds(0, 64)] = layer(unary, d // 2, near).astype(BF16)
        halo_out[d, pl.ds(64, 64)] = layer(unary, d // 2, behind).astype(BF16)
        copies.append(send_from(halo_out.at[d], halo_in.at[d], halo_ss.at[d], halo_rs.at[d], neighbour[d]))

    loads[1].wait()
    factor = jnp.exp(pot[...].astype(F32) / 64.0)
    table[...] = factor.astype(BF16)
    table_t[...] = factor.T.astype(BF16)

    def push(t, d, x, message):
        if d == 0:
            inc[t, d, x + 2] = message
        elif d == 1:
            inc[t, d, x] = message
        elif d == 2:
            inc[t, d, x + 1, pl.ds(8, 56)] = message[:56]
        elif d == 3:
            inc[t, d, x + 1, pl.ds(0, 56)] = message[8:]
        elif d == 4:
            inc[t, d, x + 1] = turn(message, 1)
        else:
            inc[t, d, x + 1] = turn(message, -1)

    def first_messages(x, _):
        value = jnp.exp(unary[x + 1] / 32.0)
        unary[x + 1] = value
        scores = dot(value, table[...])
        inv_total = 1.0 / lanes(scores)
        inv_s1[x + 1] = 1.0 / scores
        inv_t1[x + 1] = wide(inv_total)
        message = scores * (LABELS * inv_total)
        for d in range(6):
            push(0, d, x, message)
        return 0

    lax.fori_loop(0, 8, first_messages, 0, unroll=True)

    for copy in copies:
        copy.wait_recv()
    scores_in = jnp.concatenate(
        [halo_in[...].astype(F32).reshape(768, LABELS), line_in[...].reshape(96, LABELS)], axis=0
    )
    value = jnp.exp(scores_in / 32.0)
    scores = dot(value, table[...])
    inv_total = 1.0 / lanes(scores)
    ghost_u[...] = value
    ghost_is[...] = 1.0 / scores
    ghost_it[...] = wide(inv_total)
    ghost_m[...] = scores * (LABELS * inv_total)
    for d in range(6):
        face = ghost_m[pl.ds(d * 128, 64)]
        put(inc, (0, d), d // 2, d % 2 == 1, jnp.where(outside[d], 1.0, face))

    def line_of(d, e):
        return pl.ds(768 + edge_at(d, e) * 8, 8)

    for d in range(6):
        near = ghost_m[pl.ds(d * 128, 64)]
        value = ghost_u[pl.ds(d * 128, 64)] * ghost_m[pl.ds(d * 128 + 64, 64)]
        p, r = [axis for axis in range(3) if axis != d // 2]
        for e in (2 * p, 2 * p + 1):
            line = jnp.where(outside[e], 1.0, ghost_m[line_of(d, e)])
            if e % 2 == 0:
                value = value * jnp.concatenate([line, near[:56]], axis=0)
            else:
                value = value * jnp.concatenate([near[8:], line], axis=0)
        for e in (2 * r, 2 * r + 1):
            side[d, e % 2] = turn(near, 1 - 2 * (e % 2))
            line = jnp.where(outside[e], 1.0, ghost_m[line_of(d, e)])
            side[d, e % 2, pl.ds(0 if e % 2 == 0 else 7, 8, stride=8)] = line
            value = value * side[d, e % 2]
        ghost_c[pl.ds(d * 64, 64)] = value
    scores = dot(ghost_c[...], table[...])
    inv_total = 1.0 / lanes(scores)
    ghost_is2[...] = 1.0 / scores
    ghost_it2[...] = wide(inv_total)
    ghost_m2 = scores * (LABELS * inv_total)
    for t in (1, 2):
        if t == 2:
            faces = []
            for d in range(6):
                value = take(unary, (), d // 2, d % 2 == 0)
                for e in range(6):
                    if e != d ^ 1:
                        value = value * take(inc, (t - 1, e), d // 2, d % 2 == 0)
                faces.append(value.astype(BF16))
            scores = dot(jnp.concatenate(faces, axis=0), table[...])
            message = scores * (LABELS / lanes(scores))
            copies = [send(0, d, neighbour[d], message[d * 64 : d * 64 + 64]) for d in range(6)]

        def messages(x, _, t=t):
            values, _ = cavities(unary[x + 1], [inc[t - 1, d, x + 1] for d in range(6)])
            for d in range(6):
                rounded = values[d].astype(BF16)
                cav[t - 1, d, x + 1] = values[d]
                cav16[t - 1, d, x] = rounded
                scores = dot(rounded, table[...])
                inv_total = 1.0 / lanes(scores)
                inv_s[t - 1, d, x + 1] = 1.0 / scores
                inv_t[t - 1, d, x + 1] = wide(inv_total)
                push(t, d, x, scores * (LABELS * inv_total))
            return 0

        lax.fori_loop(0, 8, messages, 0, unroll=True)
        if t == 1:
            for d in range(6):
                face = ghost_m2[d * 64 : d * 64 + 64]
                put(inc, (1, d), d // 2, d % 2 == 1, jnp.where(outside[d], 1.0, face))
    for copy in copies:
        copy.wait_recv()
    for d in range(6):
        face = in_face[0, d].astype(F32)
        put(inc, (2, d), d // 2, d % 2 == 1, jnp.where(outside[d], 1.0, face))

    loads[2].wait()
    empty = jnp.zeros((64, LABELS), F32)
    for x in (0, 9):
        log_grad[x] = empty
        for t in range(2):
            whole[t, x] = empty
            for d in range(6):
                parts[t, d, x] = empty

    def beliefs(x, _):
        product = unary[x + 1]
        for d in range(6):
            product = product * inc[2, d, x + 1]
        target = bg[x].astype(F32)
        log_grad[x + 1] = target - product * (lanes(target) / lanes(product))
        return 0

    lax.fori_loop(0, 8, beliefs, 0, unroll=True)
    copies = [send(1, d, neighbour[d ^ 1], take(log_grad, (), d // 2, d % 2 == 1)) for d in range(6)]

    place = lax.rem(lax.broadcasted_iota(jnp.int32, (64, LABELS), 0), 8)
    border = jnp.zeros((8, LABELS), F32)

    def arrived(read, d, x):
        if d == 0:
            return read(d, x + 2)
        if d == 1:
            return read(d, x)
        if d == 2:
            return jnp.concatenate([read(d, x + 1)[8:], border], axis=0)
        if d == 3:
            return jnp.concatenate([border, read(d, x + 1)[:56]], axis=0)
        if d == 4:
            return jnp.where(place == 7, 0.0, turn(read(d, x + 1), -1))
        return jnp.where(place == 0, 0.0, turn(read(d, x + 1), 1))

    def last_grads(d, x):
        return log_grad[x]

    def grads_of(t):
        return lambda d, x: whole[t, x] - parts[t, d ^ 1, x]

    pair[...] = jnp.zeros_like(pair)

    def backward(t, read):
        for x in range(8):
            total = None
            for d in range(6):
                grad = arrived(read, d, x)
                score_grad = grad * inv_s[t, d, x + 1] - lanes(grad) * inv_t[t, d, x + 1]
                rounded = score_grad.astype(BF16)
                sgrad16[d, x] = rounded
                part = dot(rounded, table_t[...]) * cav[t, d, x + 1]
                parts[t, d, x + 1] = part
                total = part if total is None else total + part
            whole[t, x + 1] = total
        for d in range(6):
            pair[...] += dot_rows(
                cav16[t, d].reshape(512, LABELS), sgrad16[d].reshape(512, LABELS)
            )

    def backward_faces(t, stage):
        rounded, at = [], []
        for d in range(6):
            upper = d % 2 == 0
            grad = jnp.where(outside[d ^ 1], 0.0, in_face[stage, d].astype(F32))
            score_grad = grad * take(inv_s, (t, d), d // 2, upper)
            score_grad -= lanes(grad) * take(inv_t, (t, d), d // 2, upper)
            rounded.append(score_grad.astype(BF16))
            at.append(take(cav, (t, d), d // 2, upper))
        rounded = jnp.concatenate(rounded, axis=0)
        back = dot(rounded, table_t[...])
        for d in range(6):
            upper = d % 2 == 0
            part = back[d * 64 : d * 64 + 64] * at[d]
            put(parts, (t, d), d // 2, upper, part)
            put(whole, (t,), d // 2, upper, take(whole, (t,), d // 2, upper) + part)
        return at, rounded

    def leaving(t):
        return [
            take(whole, (t,), d // 2, d % 2 == 1) - take(parts, (t, d ^ 1), d // 2, d % 2 == 1)
            for d in range(6)
        ]

    backward(1, last_grads)
    for copy in copies:
        copy.wait_recv()
    at, rounded = backward_faces(1, 1)
    edge = leaving(1)
    copies = [send(2, d, neighbour[d ^ 1], edge[d]) for d in range(6)]
    pair[...] += dot_rows(jnp.concatenate(at, axis=0).astype(BF16), rounded)

    grad = jnp.concatenate([jnp.where(outside[d], 0.0, edge[d]) for d in range(6)], axis=0)
    score_grad = grad * ghost_is2[...] - lanes(grad) * ghost_it2[...]
    rounded = score_grad.astype(BF16)
    pair[...] += dot_rows(ghost_c[...].astype(BF16), rounded)
    beyond = dot(rounded, table_t[...]) * ghost_c[...]

    backward(0, grads_of(1))

    read = grads_of(0)

    def first_grad(x):
        grad = arrived(read, 0, x)
        for d in range(1, 6):
            grad += arrived(read, d, x)
        score_grad = grad * inv_s1[x + 1] - lanes(grad) * inv_t1[x + 1]
        return score_grad.astype(BF16)

    for x in range(8):
        sgrad16[0, x] = first_grad(x)
        cav16[0, 0, x] = unary[x + 1].astype(BF16)
    pair[...] += dot_rows(cav16[0, 0].reshape(512, LABELS), sgrad16[0].reshape(512, LABELS))

    edge = leaving(0)
    lines = [None] * len(EDGES)

    def add_line(d, e, value):
        k = edge_at(d, e)
        value = jnp.where(outside[e], 0.0, value)
        lines[k] = value if lines[k] is None else lines[k] + value

    for d in range(6):
        here = beyond[d * 64 : d * 64 + 64]
        near = jnp.where(outside[d], 0.0, edge[d])
        p, r = [axis for axis in range(3) if axis != d // 2]
        near += jnp.concatenate([here[8:], border], axis=0)
        add_line(d, 2 * p, here[:8])
        near += jnp.concatenate([border, here[:56]], axis=0)
        add_line(d, 2 * p + 1, here[56:])
        near += jnp.where(place == 7, 0.0, turn(here, -1))
        near += jnp.where(place == 0, 0.0, turn(here, 1))
        side[d, 0] = here
        add_line(d, 2 * r, side[d, 0, pl.ds(0, 8, stride=8)])
        add_line(d, 2 * r + 1, side[d, 0, pl.ds(7, 8, stride=8)])
        ghost_g[pl.ds(d * 128, 64)] = near
        ghost_g[pl.ds(d * 128 + 64, 64)] = here
    for k in range(len(EDGES)):
        ghost_g[pl.ds(768 + k * 8, 8)] = lines[k]
    grad = ghost_g[...]
    score_grad = grad * ghost_is[...] - lanes(grad) * ghost_it[...]
    pair[...] += dot_rows(ghost_u[...].astype(BF16), score_grad.astype(BF16))

    height = LABELS // firsts

    def rows_of(j):
        return pl.ds(pl.multiple_of(j * height, height), height)

    sends = [
        send_from(
            pair.at[rows_of(lax.rem(first_id + k, firsts))], part1.at[k - 1],
            s1_ss.at[k - 1], s1_rs.at[k - 1], first_peer(k),
        )
        for k in range(1, firsts)
    ]

    for copy in copies:
        copy.wait_recv()
    backward_faces(0, 2)
    edge = leaving(0)
    copies = [send(3, d, neighbour[d ^ 1], edge[d]) for d in range(6)]

    for copy in sends:
        copy.wait_recv()
    mine = pair[rows_of(first_id)]
    for k in range(1, firsts):
        mine += part1[k - 1]
    part2[second_id] = mine.astype(BF16)
    own = part2.at[second_id]
    sends = [
        send_from(own, own, s2_ss.at[k - 1], s2_rs.at[k - 1], second_peer(k))
        for k in range(1, seconds)
    ]
    for x in range(8):
        back = dot(first_grad(x), table_t[...]) * unary[x + 1]
        ug[x + 1] = log_grad[x + 1] + whole[1, x + 1] + whole[0, x + 1] + back
    for copy in copies:
        copy.wait_recv()
    rounded = []
    for d in range(6):
        upper = d % 2 == 0
        grad = jnp.where(outside[d ^ 1], 0.0, in_face[3, d].astype(F32))
        score_grad = grad * take(inv_s1, (), d // 2, upper)
        score_grad -= lanes(grad) * take(inv_t1, (), d // 2, upper)
        rounded.append(score_grad.astype(BF16))
    back = dot(jnp.concatenate(rounded, axis=0), table_t[...])
    for d in range(6):
        upper = d % 2 == 0
        part = back[d * 64 : d * 64 + 64] * take(unary, (), d // 2, upper)
        put(ug, (), d // 2, upper, take(ug, (), d // 2, upper) + part)
    store = pltpu.make_async_copy(ug.at[pl.ds(1, 8)], ug_out, out_sem.at[0])
    store.start()

    for copy in sends:
        copy.wait_recv()
    final[rows_of(first_id)] = jnp.sum(part2[...].astype(F32), axis=0)
    here = final.at[rows_of(first_id)]
    sends = [
        send_from(here, here, s3_ss.at[k - 1], s3_rs.at[k - 1], first_peer(k))
        for k in range(1, firsts)
    ]
    for copy in sends:
        copy.wait_recv()
    factor = jnp.exp(pot[...].astype(F32) / 64.0)
    for copy in started:
        copy.wait_send()
    pair[...] = factor * final[...] * (LABELS / math.sqrt(CELLS))
    store2 = pltpu.make_async_copy(pair, pg_out, out_sem.at[1])
    store2.start()
    store.wait()
    store2.wait()


def on_device(unary_q, potential_q, belief_grad):
    slabs = (8, 64, LABELS)
    padded = (10, 64, LABELS)
    firsts = lax.axis_size("gx") * 2
    seconds = lax.axis_size("gy") * (lax.axis_size("gz") // 2)
    height = LABELS // firsts
    vmem, dma = pltpu.VMEM, pltpu.SemaphoreType.DMA
    unary_grad, potential_grad = pl.pallas_call(
        kernel,
        out_shape=(
            jax.ShapeDtypeStruct(slabs, F32),
            jax.ShapeDtypeStruct((LABELS, LABELS), F32),
        ),
        in_specs=[pl.BlockSpec(memory_space=pltpu.HBM)] * 3,
        out_specs=(pl.BlockSpec(memory_space=pltpu.HBM),) * 2,
        scratch_shapes=[
            vmem(slabs, jnp.int32),
            vmem((LABELS, LABELS), jnp.int32),
            vmem(slabs, BF16),
            vmem((LABELS, LABELS), BF16),
            vmem((LABELS, LABELS), BF16),
            vmem(padded, F32),
            vmem((3, 6, *padded), F32),
            vmem((2, 6, *padded), F32),
            vmem((2, 6, *slabs), BF16),
            vmem((2, 6, *padded), F32),
            vmem((2, 6, *padded), F32),
            vmem(padded, F32),
            vmem(padded, F32),
            vmem(padded, F32),
            vmem((2, 6, *padded), F32),
            vmem((2, *padded), F32),
            vmem((6, *slabs), BF16),
            vmem((LABELS, LABELS), F32),
            vmem(padded, F32),
            vmem((4, 6, 64, LABELS), BF16),
            vmem((4, 6, 64, LABELS), BF16),
            *[vmem((GHOSTS, LABELS), F32)] * 5,
            *[vmem((384, LABELS), F32)] * 3,
            vmem((6, 2, 64, LABELS), F32),
            vmem((len(EDGES), 8, LABELS), F32),
            vmem((len(EDGES), 8, LABELS), F32),
            vmem((6, 128, LABELS), BF16),
            vmem((6, 128, LABELS), BF16),
            vmem((firsts - 1, height, LABELS), F32),
            vmem((seconds, height, LABELS), BF16),
            vmem((LABELS, LABELS), F32),
            dma((3,)),
            dma((2,)),
            dma((4, 6)),
            dma((4, 6)),
            dma((6,)),
            dma((6,)),
            dma((len(EDGES),)),
            dma((len(EDGES),)),
            dma((firsts - 1,)),
            dma((firsts - 1,)),
            dma((seconds - 1,)),
            dma((seconds - 1,)),
            dma((firsts - 1,)),
            dma((firsts - 1,)),
        ],
        compiler_params=pltpu.CompilerParams(
            collective_id=0, has_side_effects=True, vmem_limit_bytes=60 * 2**20
        ),
    )(unary_q.reshape(slabs), potential_q, belief_grad.reshape(slabs))
    return unary_grad.reshape(unary_q.shape), potential_grad


def solution(mesh):
    return jax.shard_map(
        on_device,
        mesh=mesh,
        in_specs=(P("gx", "gy", "gz", None), P(), P("gx", "gy", "gz", None)),
        out_specs=(P("gx", "gy", "gz", None), P()),
        check_vma=False,
    )
```

```python
import math

import jax
import jax.numpy as jnp
from jax import lax
from jax.experimental import pallas as pl
from jax.experimental.pallas import tpu as pltpu
from jax.sharding import PartitionSpec as P

LABELS = 128
CELLS = 131072
AXES = ("gx", "gy", "gz")
F32 = jnp.float32
BF16 = jnp.bfloat16
MESH = pl.DeviceIdType.MESH
EDGES = [(d, e) for d in range(6) for e in range(d + 1, 6) if d // 2 != e // 2]
GHOSTS = 6 * 128 + len(EDGES) * 8


def take(ref, lead, axis, upper):
    if axis == 0:
        return ref[(*lead, 8 if upper else 1)]
    if axis == 1:
        rows = pl.ds(56 if upper else 0, 8)
    else:
        rows = pl.ds(7 if upper else 0, 8, stride=8)
    return ref[(*lead, pl.ds(1, 8), rows)].reshape(64, LABELS)


def layer(ref, axis, index):
    if axis == 0:
        return ref[index + 1]
    if axis == 1:
        rows = pl.ds(index * 8, 8)
    else:
        rows = pl.ds(index, 8, stride=8)
    return ref[pl.ds(1, 8), rows].reshape(64, LABELS)


def edge_at(d, e):
    return EDGES.index((d, e) if d < e else (e, d))


def put(ref, lead, axis, upper, value):
    if axis == 0:
        ref[(*lead, 8 if upper else 1)] = value
        return
    if axis == 1:
        rows = pl.ds(56 if upper else 0, 8)
    else:
        rows = pl.ds(7 if upper else 0, 8, stride=8)
    ref[(*lead, pl.ds(1, 8), rows)] = value.reshape(8, 8, LABELS)


def turn(value, steps):
    rows = value.shape[0]
    tiles = value.reshape(rows // 8, 8, LABELS)
    return pltpu.roll(tiles, steps % 8, 1).reshape(rows, LABELS)


def dot(a, b):
    return jnp.dot(a.astype(BF16), b, preferred_element_type=F32)


def dot_rows(a, b):
    return lax.dot_general(a, b, (((0,), (0,)), ((), ())), preferred_element_type=F32)


def lanes(value):
    return jnp.sum(value, axis=-1, keepdims=True)


def wide(value):
    return jnp.broadcast_to(value, (value.shape[0], LABELS))


def cavities(unary, incoming):
    xs = incoming[0] * incoming[1]
    ys = incoming[2] * incoming[3]
    zs = incoming[4] * incoming[5]
    ux = unary * xs
    no_z = ux * ys
    no_y = ux * zs
    no_x = unary * ys * zs
    rest = (no_x, no_x, no_y, no_y, no_z, no_z)
    return [rest[d] * incoming[d] for d in range(6)], no_z * zs


def kernel(
    q_hbm, pot_hbm, bg_hbm, ug_out, pg_out,
    q, pot, bg, table, table_t, unary, inc, cav, cav16, inv_s, inv_t, inv_s1, inv_t1,
    log_grad, parts, whole, sgrad16, pair, ug, out_face, in_face, ghost_u, ghost_is, ghost_it, ghost_m, ghost_g,
    ghost_c, ghost_is2, ghost_it2, side, line_out, line_in, halo_out, halo_in,
    part1, part2, final,
    in_sem, out_sem, face_ss, face_rs, halo_ss, halo_rs, line_ss, line_rs, s1_ss, s1_rs, s2_ss, s2_rs, s3_ss, s3_rs,
):
    gx, gy, gz = (lax.axis_index(a) for a in AXES)
    nx, ny, nz = (lax.axis_size(a) for a in AXES)

    def beside(axis, step):
        at = [gx, gy, gz]
        size = (nx, ny, nz)[axis]
        at[axis] = lax.rem(at[axis] + step + size, size)
        return tuple(at)

    neighbour = [beside(d // 2, 1 - 2 * (d % 2)) for d in range(6)]
    across = []
    for d, e in EDGES:
        at = list(neighbour[d])
        at[e // 2] = neighbour[e][e // 2]
        across.append(tuple(at))
    at_low = (gx == 0, gy == 0, gz == 0)
    at_high = (gx == nx - 1, gy == ny - 1, gz == nz - 1)
    outside = [(at_high if d % 2 else at_low)[d // 2] for d in range(6)]

    core = lax.rem(gz, 2)
    first_id = gx * 2 + core
    firsts = nx * 2
    second_id = gy * (nz // 2) + gz // 2
    seconds = ny * (nz // 2)

    def first_peer(k):
        j = lax.rem(first_id + k, firsts)
        return (j // 2, gy, gz - core + lax.rem(j, 2))

    def second_peer(k):
        j = lax.rem(second_id + k, seconds)
        return (gx, j // (nz // 2), lax.rem(j, nz // 2) * 2 + core)

    loads = [
        pltpu.make_async_copy(q_hbm, q, in_sem.at[0]),
        pltpu.make_async_copy(pot_hbm, pot, in_sem.at[1]),
        pltpu.make_async_copy(bg_hbm, bg, in_sem.at[2]),
    ]
    for load in loads:
        load.start()
    barrier = pltpu.get_barrier_semaphore()
    met = 0
    for place in neighbour + across:
        pl.semaphore_signal(barrier, inc=1, device_id=place, device_id_type=MESH)
        met += 1
    for dy in (-1, 1):
        for dz in (-2, 2):
            place = (gx, lax.rem(gy + dy + ny, ny), lax.rem(gz + dz + nz, nz))
            pl.semaphore_signal(barrier, inc=1, device_id=place, device_id_type=MESH)
            met += 1

    started = []

    def send(stage, slot, target, value):
        out_face[stage, slot] = value.astype(BF16)
        copy = pltpu.make_async_remote_copy(
            src_ref=out_face.at[stage, slot],
            dst_ref=in_face.at[stage, slot],
            send_sem=face_ss.at[stage, slot],
            recv_sem=face_rs.at[stage, slot],
            device_id=target,
            device_id_type=MESH,
        )
        copy.start()
        started.append(copy)
        return copy

    loads[0].wait()

    def factors(x, _):
        unary[x + 1] = q[x].astype(F32)
        return 0

    lax.fori_loop(0, 8, factors, 0, unroll=True)
    pl.semaphore_wait(barrier, met)
    copies = []

    def send_from(src, dst, ss, rs, target):
        copy = pltpu.make_async_remote_copy(
            src_ref=src, dst_ref=dst, send_sem=ss, recv_sem=rs, device_id=target, device_id_type=MESH
        )
        copy.start()
        started.append(copy)
        return copy

    for k, (d, e) in enumerate(EDGES):
        near = [7 if f % 2 == 0 else 0 for f in (d, e)]
        if (d // 2, e // 2) == (0, 1):
            line_out[k] = unary[near[0] + 1, pl.ds(near[1] * 8, 8)]
        elif (d // 2, e // 2) == (0, 2):
            line_out[k] = unary[near[0] + 1, pl.ds(near[1], 8, stride=8)]
        else:
            for x in range(8):
                row = pl.ds(near[0] * 8 + near[1], 1)
                line_out[k, pl.ds(x, 1)] = unary[x + 1, row]
        copies.append(send_from(line_out.at[k], line_in.at[k], line_ss.at[k], line_rs.at[k], across[k]))
    for d in range(6):
        near, behind = (7, 6) if d % 2 == 0 else (0, 1)
        halo_out[d, pl.ds(0, 64)] = layer(unary, d // 2, near).astype(BF16)
        halo_out[d, pl.ds(64, 64)] = layer(unary, d // 2, behind).astype(BF16)
        copies.append(send_from(halo_out.at[d], halo_in.at[d], halo_ss.at[d], halo_rs.at[d], neighbour[d]))

    loads[1].wait()
    factor = jnp.exp(pot[...].astype(F32) / 64.0)
    table[...] = factor.astype(BF16)
    table_t[...] = factor.T.astype(BF16)

    def push(t, d, x, message):
        if d == 0:
            inc[t, d, x + 2] = message
        elif d == 1:
            inc[t, d, x] = message
        elif d == 2:
            inc[t, d, x + 1, pl.ds(8, 56)] = message[:56]
        elif d == 3:
            inc[t, d, x + 1, pl.ds(0, 56)] = message[8:]
        elif d == 4:
            inc[t, d, x + 1] = turn(message, 1)
        else:
            inc[t, d, x + 1] = turn(message, -1)

    def first_messages(x, _):
        value = jnp.exp(unary[x + 1] / 32.0)
        unary[x + 1] = value
        scores = dot(value, table[...])
        inv_total = 1.0 / lanes(scores)
        inv_s1[x + 1] = 1.0 / scores
        inv_t1[x + 1] = wide(inv_total)
        message = scores * (LABELS * inv_total)
        for d in range(6):
            push(0, d, x, message)
        return 0

    lax.fori_loop(0, 8, first_messages, 0, unroll=True)

    for copy in copies:
        copy.wait_recv()
    scores_in = jnp.concatenate(
        [halo_in[...].astype(F32).reshape(768, LABELS), line_in[...].reshape(96, LABELS)], axis=0
    )
    value = jnp.exp(scores_in / 32.0)
    scores = dot(value, table[...])
    inv_total = 1.0 / lanes(scores)
    ghost_u[...] = value
    ghost_is[...] = 1.0 / scores
    ghost_it[...] = wide(inv_total)
    ghost_m[...] = scores * (LABELS * inv_total)
    for d in range(6):
        face = ghost_m[pl.ds(d * 128, 64)]
        put(inc, (0, d), d // 2, d % 2 == 1, jnp.where(outside[d], 1.0, face))

    def line_of(d, e):
        return pl.ds(768 + edge_at(d, e) * 8, 8)

    for d in range(6):
        near = ghost_m[pl.ds(d * 128, 64)]
        value = ghost_u[pl.ds(d * 128, 64)] * ghost_m[pl.ds(d * 128 + 64, 64)]
        p, r = [axis for axis in range(3) if axis != d // 2]
        for e in (2 * p, 2 * p + 1):
            line = jnp.where(outside[e], 1.0, ghost_m[line_of(d, e)])
            if e % 2 == 0:
                value = value * jnp.concatenate([line, near[:56]], axis=0)
            else:
                value = value * jnp.concatenate([near[8:], line], axis=0)
        for e in (2 * r, 2 * r + 1):
            side[d, e % 2] = turn(near, 1 - 2 * (e % 2))
            line = jnp.where(outside[e], 1.0, ghost_m[line_of(d, e)])
            side[d, e % 2, pl.ds(0 if e % 2 == 0 else 7, 8, stride=8)] = line
            value = value * side[d, e % 2]
        ghost_c[pl.ds(d * 64, 64)] = value
    scores = dot(ghost_c[...], table[...])
    inv_total = 1.0 / lanes(scores)
    ghost_is2[...] = 1.0 / scores
    ghost_it2[...] = wide(inv_total)
    ghost_m2 = scores * (LABELS * inv_total)
    for t in (1, 2):
        if t == 2:
            faces = []
            for d in range(6):
                value = take(unary, (), d // 2, d % 2 == 0)
                for e in range(6):
                    if e != d ^ 1:
                        value = value * take(inc, (t - 1, e), d // 2, d % 2 == 0)
                faces.append(value.astype(BF16))
            scores = dot(jnp.concatenate(faces, axis=0), table[...])
            message = scores * (LABELS / lanes(scores))
            copies = [send(0, d, neighbour[d], message[d * 64 : d * 64 + 64]) for d in range(6)]

        def messages(x, _, t=t):
            values, _ = cavities(unary[x + 1], [inc[t - 1, d, x + 1] for d in range(6)])
            for d in range(6):
                rounded = values[d].astype(BF16)
                cav[t - 1, d, x + 1] = values[d]
                cav16[t - 1, d, x] = rounded
                scores = dot(rounded, table[...])
                inv_total = 1.0 / lanes(scores)
                inv_s[t - 1, d, x + 1] = 1.0 / scores
                inv_t[t - 1, d, x + 1] = wide(inv_total)
                push(t, d, x, scores * (LABELS * inv_total))
            return 0

        lax.fori_loop(0, 8, messages, 0, unroll=True)
        if t == 1:
            for d in range(6):
                face = ghost_m2[d * 64 : d * 64 + 64]
                put(inc, (1, d), d // 2, d % 2 == 1, jnp.where(outside[d], 1.0, face))
    for copy in copies:
        copy.wait_recv()
    for d in range(6):
        face = in_face[0, d].astype(F32)
        put(inc, (2, d), d // 2, d % 2 == 1, jnp.where(outside[d], 1.0, face))

    loads[2].wait()
    empty = jnp.zeros((64, LABELS), F32)
    for x in (0, 9):
        log_grad[x] = empty
        for t in range(2):
            whole[t, x] = empty
            for d in range(6):
                parts[t, d, x] = empty

    def beliefs(x, _):
        product = unary[x + 1]
        for d in range(6):
            product = product * inc[2, d, x + 1]
        target = bg[x].astype(F32)
        log_grad[x + 1] = target - product * (lanes(target) / lanes(product))
        return 0

    lax.fori_loop(0, 8, beliefs, 0, unroll=True)
    copies = [send(1, d, neighbour[d ^ 1], take(log_grad, (), d // 2, d % 2 == 1)) for d in range(6)]

    place = lax.rem(lax.broadcasted_iota(jnp.int32, (64, LABELS), 0), 8)
    border = jnp.zeros((8, LABELS), F32)

    def arrived(read, d, x):
        if d == 0:
            return read(d, x + 2)
        if d == 1:
            return read(d, x)
        if d == 2:
            return jnp.concatenate([read(d, x + 1)[8:], border], axis=0)
        if d == 3:
            return jnp.concatenate([border, read(d, x + 1)[:56]], axis=0)
        if d == 4:
            return jnp.where(place == 7, 0.0, turn(read(d, x + 1), -1))
        return jnp.where(place == 0, 0.0, turn(read(d, x + 1), 1))

    def last_grads(d, x):
        return log_grad[x]

    def grads_of(t):
        return lambda d, x: whole[t, x] - parts[t, d ^ 1, x]

    pair[...] = jnp.zeros_like(pair)

    def backward(t, read):
        for x in range(8):
            total = None
            for d in range(6):
                grad = arrived(read, d, x)
                score_grad = grad * inv_s[t, d, x + 1] - lanes(grad) * inv_t[t, d, x + 1]
                rounded = score_grad.astype(BF16)
                sgrad16[d, x] = rounded
                part = dot(rounded, table_t[...]) * cav[t, d, x + 1]
                parts[t, d, x + 1] = part
                total = part if total is None else total + part
            whole[t, x + 1] = total
        for d in range(6):
            pair[...] += dot_rows(
                cav16[t, d].reshape(512, LABELS), sgrad16[d].reshape(512, LABELS)
            )

    def backward_faces(t, stage):
        rounded, at = [], []
        for d in range(6):
            upper = d % 2 == 0
            grad = jnp.where(outside[d ^ 1], 0.0, in_face[stage, d].astype(F32))
            score_grad = grad * take(inv_s, (t, d), d // 2, upper)
            score_grad -= lanes(grad) * take(inv_t, (t, d), d // 2, upper)
            rounded.append(score_grad.astype(BF16))
            at.append(take(cav, (t, d), d // 2, upper))
        rounded = jnp.concatenate(rounded, axis=0)
        back = dot(rounded, table_t[...])
        for d in range(6):
            upper = d % 2 == 0
            part = back[d * 64 : d * 64 + 64] * at[d]
            put(parts, (t, d), d // 2, upper, part)
            put(whole, (t,), d // 2, upper, take(whole, (t,), d // 2, upper) + part)
        return at, rounded

    def leaving(t):
        return [
            take(whole, (t,), d // 2, d % 2 == 1) - take(parts, (t, d ^ 1), d // 2, d % 2 == 1)
            for d in range(6)
        ]

    backward(1, last_grads)
    for copy in copies:
        copy.wait_recv()
    at, rounded = backward_faces(1, 1)
    edge = leaving(1)
    copies = [send(2, d, neighbour[d ^ 1], edge[d]) for d in range(6)]
    pair[...] += dot_rows(jnp.concatenate(at, axis=0).astype(BF16), rounded)

    grad = jnp.concatenate([jnp.where(outside[d], 0.0, edge[d]) for d in range(6)], axis=0)
    score_grad = grad * ghost_is2[...] - lanes(grad) * ghost_it2[...]
    rounded = score_grad.astype(BF16)
    pair[...] += dot_rows(ghost_c[...].astype(BF16), rounded)
    beyond = dot(rounded, table_t[...]) * ghost_c[...]

    backward(0, grads_of(1))

    read = grads_of(0)

    def first_grad(x):
        grad = arrived(read, 0, x)
        for d in range(1, 6):
            grad += arrived(read, d, x)
        score_grad = grad * inv_s1[x + 1] - lanes(grad) * inv_t1[x + 1]
        return score_grad.astype(BF16)

    for x in range(8):
        sgrad16[0, x] = first_grad(x)
        cav16[0, 0, x] = unary[x + 1].astype(BF16)
    pair[...] += dot_rows(cav16[0, 0].reshape(512, LABELS), sgrad16[0].reshape(512, LABELS))

    edge = leaving(0)
    lines = [None] * len(EDGES)

    def add_line(d, e, value):
        k = edge_at(d, e)
        value = jnp.where(outside[e], 0.0, value)
        lines[k] = value if lines[k] is None else lines[k] + value

    for d in range(6):
        here = beyond[d * 64 : d * 64 + 64]
        near = jnp.where(outside[d], 0.0, edge[d])
        p, r = [axis for axis in range(3) if axis != d // 2]
        near += jnp.concatenate([here[8:], border], axis=0)
        add_line(d, 2 * p, here[:8])
        near += jnp.concatenate([border, here[:56]], axis=0)
        add_line(d, 2 * p + 1, here[56:])
        near += jnp.where(place == 7, 0.0, turn(here, -1))
        near += jnp.where(place == 0, 0.0, turn(here, 1))
        side[d, 0] = here
        add_line(d, 2 * r, side[d, 0, pl.ds(0, 8, stride=8)])
        add_line(d, 2 * r + 1, side[d, 0, pl.ds(7, 8, stride=8)])
        ghost_g[pl.ds(d * 128, 64)] = near
        ghost_g[pl.ds(d * 128 + 64, 64)] = here
    for k in range(len(EDGES)):
        ghost_g[pl.ds(768 + k * 8, 8)] = lines[k]
    grad = ghost_g[...]
    score_grad = grad * ghost_is[...] - lanes(grad) * ghost_it[...]
    pair[...] += dot_rows(ghost_u[...].astype(BF16), score_grad.astype(BF16))

    height = LABELS // firsts

    def rows_of(j):
        return pl.ds(pl.multiple_of(j * height, height), height)

    sends = [
        send_from(
            pair.at[rows_of(lax.rem(first_id + k, firsts))], part1.at[k - 1],
            s1_ss.at[k - 1], s1_rs.at[k - 1], first_peer(k),
        )
        for k in range(1, firsts)
    ]

    for copy in copies:
        copy.wait_recv()
    backward_faces(0, 2)
    edge = leaving(0)
    copies = [send(3, d, neighbour[d ^ 1], edge[d]) for d in range(6)]

    for copy in sends:
        copy.wait_recv()
    mine = pair[rows_of(first_id)]
    for k in range(1, firsts):
        mine += part1[k - 1]
    part2[second_id] = mine.astype(BF16)
    own = part2.at[second_id]
    sends = [
        send_from(own, own, s2_ss.at[k - 1], s2_rs.at[k - 1], second_peer(k))
        for k in range(1, seconds)
    ]
    for x in range(8):
        back = dot(first_grad(x), table_t[...]) * unary[x + 1]
        ug[x + 1] = log_grad[x + 1] + whole[1, x + 1] + whole[0, x + 1] + back
    for copy in copies:
        copy.wait_recv()
    rounded = []
    for d in range(6):
        upper = d % 2 == 0
        grad = jnp.where(outside[d ^ 1], 0.0, in_face[3, d].astype(F32))
        score_grad = grad * take(inv_s1, (), d // 2, upper)
        score_grad -= lanes(grad) * take(inv_t1, (), d // 2, upper)
        rounded.append(score_grad.astype(BF16))
    back = dot(jnp.concatenate(rounded, axis=0), table_t[...])
    for d in range(6):
        upper = d % 2 == 0
        part = back[d * 64 : d * 64 + 64] * take(unary, (), d // 2, upper)
        put(ug, (), d // 2, upper, take(ug, (), d // 2, upper) + part)
    store = pltpu.make_async_copy(ug.at[pl.ds(1, 8)], ug_out, out_sem.at[0])
    store.start()

    for copy in sends:
        copy.wait_recv()
    final[rows_of(first_id)] = jnp.sum(part2[...].astype(F32), axis=0)
    here = final.at[rows_of(first_id)]
    sends = [
        send_from(here, here, s3_ss.at[k - 1], s3_rs.at[k - 1], first_peer(k))
        for k in range(1, firsts)
    ]
    for copy in sends:
        copy.wait_recv()
    factor = jnp.exp(pot[...].astype(F32) / 64.0)
    for copy in started:
        copy.wait_send()
    pair[...] = factor * final[...] * (LABELS / math.sqrt(CELLS))
    store2 = pltpu.make_async_copy(pair, pg_out, out_sem.at[1])
    store2.start()
    store.wait()
    store2.wait()


def finish(ug, pg, ug_out, pg_out, ug_held, pg_held, sem):
    moves = [(pg, pg_held, pg_out)]
    for x in range(0, 8, 4):
        part = pl.ds(x, 4)
        moves.append((ug.at[part], ug_held.at[part], ug_out.at[part]))
    loads = [pltpu.make_async_copy(a, b, sem.at[0, k]) for k, (a, b, c) in enumerate(moves)]
    stores = [pltpu.make_async_copy(b, c, sem.at[1, k]) for k, (a, b, c) in enumerate(moves)]
    for load in loads:
        load.start()
    for load, store in zip(loads, stores):
        load.wait()
        store.start()
    for store in stores:
        store.wait()


def on_device(unary_q, potential_q, belief_grad):
    slabs = (8, 64, LABELS)
    padded = (10, 64, LABELS)
    firsts = lax.axis_size("gx") * 2
    seconds = lax.axis_size("gy") * (lax.axis_size("gz") // 2)
    height = LABELS // firsts
    vmem, dma = pltpu.VMEM, pltpu.SemaphoreType.DMA
    unary_grad, potential_grad = pl.pallas_call(
        kernel,
        out_shape=(
            jax.ShapeDtypeStruct(slabs, F32),
            jax.ShapeDtypeStruct((LABELS, LABELS), F32),
        ),
        in_specs=[pl.BlockSpec(memory_space=pltpu.HBM)] * 3,
        out_specs=(pl.BlockSpec(memory_space=pltpu.HBM),) * 2,
        scratch_shapes=[
            vmem(slabs, jnp.int32),
            vmem((LABELS, LABELS), jnp.int32),
            vmem(slabs, BF16),
            vmem((LABELS, LABELS), BF16),
            vmem((LABELS, LABELS), BF16),
            vmem(padded, F32),
            vmem((3, 6, *padded), F32),
            vmem((2, 6, *padded), F32),
            vmem((2, 6, *slabs), BF16),
            vmem((2, 6, *padded), F32),
            vmem((2, 6, *padded), F32),
            vmem(padded, F32),
            vmem(padded, F32),
            vmem(padded, F32),
            vmem((2, 6, *padded), F32),
            vmem((2, *padded), F32),
            vmem((6, *slabs), BF16),
            vmem((LABELS, LABELS), F32),
            vmem(padded, F32),
            vmem((4, 6, 64, LABELS), BF16),
            vmem((4, 6, 64, LABELS), BF16),
            *[vmem((GHOSTS, LABELS), F32)] * 5,
            *[vmem((384, LABELS), F32)] * 3,
            vmem((6, 2, 64, LABELS), F32),
            vmem((len(EDGES), 8, LABELS), F32),
            vmem((len(EDGES), 8, LABELS), F32),
            vmem((6, 128, LABELS), BF16),
            vmem((6, 128, LABELS), BF16),
            vmem((firsts - 1, height, LABELS), F32),
            vmem((seconds, height, LABELS), BF16),
            vmem((LABELS, LABELS), F32),
            dma((3,)),
            dma((2,)),
            dma((4, 6)),
            dma((4, 6)),
            dma((6,)),
            dma((6,)),
            dma((len(EDGES),)),
            dma((len(EDGES),)),
            dma((firsts - 1,)),
            dma((firsts - 1,)),
            dma((seconds - 1,)),
            dma((seconds - 1,)),
            dma((firsts - 1,)),
            dma((firsts - 1,)),
        ],
        compiler_params=pltpu.CompilerParams(
            collective_id=0, has_side_effects=True, vmem_limit_bytes=60 * 2**20
        ),
    )(unary_q.reshape(slabs), potential_q, belief_grad.reshape(slabs))
    unary_grad, potential_grad = pl.pallas_call(
        finish,
        out_shape=(
            jax.ShapeDtypeStruct(slabs, F32),
            jax.ShapeDtypeStruct((LABELS, LABELS), F32),
        ),
        in_specs=[pl.BlockSpec(memory_space=pltpu.HBM)] * 2,
        out_specs=(pl.BlockSpec(memory_space=pltpu.HBM),) * 2,
        scratch_shapes=[vmem(slabs, F32), vmem((LABELS, LABELS), F32), dma((2, 3))],
    )(unary_grad, potential_grad)
    return unary_grad.reshape(unary_q.shape), potential_grad


def solution(mesh):
    return jax.shard_map(
        on_device,
        mesh=mesh,
        in_specs=(P("gx", "gy", "gz", None), P(), P("gx", "gy", "gz", None)),
        out_specs=(P("gx", "gy", "gz", None), P()),
        check_vma=False,
    )
```

```python
import math

import jax
import jax.numpy as jnp
from jax import lax
from jax.experimental import pallas as pl
from jax.experimental.pallas import tpu as pltpu
from jax.sharding import PartitionSpec as P

LABELS = 128
CELLS = 131072
AXES = ("gx", "gy", "gz")
F32 = jnp.float32
BF16 = jnp.bfloat16
MESH = pl.DeviceIdType.MESH
EDGES = [(d, e) for d in range(6) for e in range(d + 1, 6) if d // 2 != e // 2]
GHOSTS = 6 * 128 + len(EDGES) * 8


def take(ref, lead, axis, upper):
    if axis == 0:
        return ref[(*lead, 8 if upper else 1)]
    if axis == 1:
        rows = pl.ds(56 if upper else 0, 8)
    else:
        rows = pl.ds(7 if upper else 0, 8, stride=8)
    return ref[(*lead, pl.ds(1, 8), rows)].reshape(64, LABELS)


def layer(ref, axis, index):
    if axis == 0:
        return ref[index + 1]
    if axis == 1:
        rows = pl.ds(index * 8, 8)
    else:
        rows = pl.ds(index, 8, stride=8)
    return ref[pl.ds(1, 8), rows].reshape(64, LABELS)


def edge_at(d, e):
    return EDGES.index((d, e) if d < e else (e, d))


def put(ref, lead, axis, upper, value):
    if axis == 0:
        ref[(*lead, 8 if upper else 1)] = value
        return
    if axis == 1:
        rows = pl.ds(56 if upper else 0, 8)
    else:
        rows = pl.ds(7 if upper else 0, 8, stride=8)
    ref[(*lead, pl.ds(1, 8), rows)] = value.reshape(8, 8, LABELS)


def turn(value, steps):
    rows = value.shape[0]
    tiles = value.reshape(rows // 8, 8, LABELS)
    return pltpu.roll(tiles, steps % 8, 1).reshape(rows, LABELS)


def dot(a, b):
    return jnp.dot(a.astype(BF16), b, preferred_element_type=F32)


def dot_rows(a, b):
    return lax.dot_general(a, b, (((0,), (0,)), ((), ())), preferred_element_type=F32)


def lanes(value):
    return jnp.sum(value, axis=-1, keepdims=True)


def wide(value):
    return jnp.broadcast_to(value, (value.shape[0], LABELS))


def cavities(unary, incoming):
    xs = incoming[0] * incoming[1]
    ys = incoming[2] * incoming[3]
    zs = incoming[4] * incoming[5]
    ux = unary * xs
    no_z = ux * ys
    no_y = ux * zs
    no_x = unary * ys * zs
    rest = (no_x, no_x, no_y, no_y, no_z, no_z)
    return [rest[d] * incoming[d] for d in range(6)], no_z * zs


def kernel(
    q_hbm, pot_hbm, bg_hbm, ug_out, pg_out,
    q, pot, bg, table, table_t, unary, inc, cav, cav16, inv_s, inv_t, inv_s1, inv_t1,
    log_grad, parts, whole, sgrad16, pair, ug, out_face, in_face, ghost_u, ghost_is, ghost_it, ghost_m, ghost_g,
    ghost_c, ghost_is2, ghost_it2, side, line_out, line_in, halo_out, halo_in,
    part1, part2, final,
    in_sem, out_sem, face_ss, face_rs, halo_ss, halo_rs, line_ss, line_rs, s1_ss, s1_rs, s2_ss, s2_rs, s3_ss, s3_rs,
):
    gx, gy, gz = (lax.axis_index(a) for a in AXES)
    nx, ny, nz = (lax.axis_size(a) for a in AXES)

    def beside(axis, step):
        at = [gx, gy, gz]
        size = (nx, ny, nz)[axis]
        at[axis] = lax.rem(at[axis] + step + size, size)
        return tuple(at)

    neighbour = [beside(d // 2, 1 - 2 * (d % 2)) for d in range(6)]
    across = []
    for d, e in EDGES:
        at = list(neighbour[d])
        at[e // 2] = neighbour[e][e // 2]
        across.append(tuple(at))
    at_low = (gx == 0, gy == 0, gz == 0)
    at_high = (gx == nx - 1, gy == ny - 1, gz == nz - 1)
    outside = [(at_high if d % 2 else at_low)[d // 2] for d in range(6)]

    core = lax.rem(gz, 2)
    first_id = gx * 2 + core
    firsts = nx * 2
    second_id = gy * (nz // 2) + gz // 2
    seconds = ny * (nz // 2)

    xs = [lax.rem(gx + step, nx) for step in range(nx)]
    ys = [lax.rem(gy + step, ny) for step in range(ny)]
    zs = [lax.rem(gz + step, nz) for step in range(0, nz, 2)]
    other = 1 - core
    first_peers = [
        ((x, gy, gz + flip * (other - core)), x * 2 + (other if flip else core))
        for x in xs for flip in range(2)
    ][1:]
    steps = [(j, k) for j in range(ny) for k in range(nz // 2)][1:]
    steps.sort(key=lambda at: -2 * min(at[1], nz // 2 - at[1]) - min(at[0] % 4, 4 - at[0] % 4))
    second_peers = [(gx, ys[j], zs[k]) for j, k in steps]

    loads = [
        pltpu.make_async_copy(q_hbm, q, in_sem.at[0]),
        pltpu.make_async_copy(pot_hbm, pot, in_sem.at[1]),
        pltpu.make_async_copy(bg_hbm, bg, in_sem.at[2]),
    ]
    for load in loads:
        load.start()
    barrier = pltpu.get_barrier_semaphore()
    met = 0
    for place in neighbour + across:
        pl.semaphore_signal(barrier, inc=1, device_id=place, device_id_type=MESH)
        met += 1
    for dy in (-1, 1):
        for dz in (-2, 2):
            place = (gx, lax.rem(gy + dy + ny, ny), lax.rem(gz + dz + nz, nz))
            pl.semaphore_signal(barrier, inc=1, device_id=place, device_id_type=MESH)
            met += 1

    started = []

    def send(stage, slot, target, value):
        out_face[stage, slot] = value.astype(BF16)
        copy = pltpu.make_async_remote_copy(
            src_ref=out_face.at[stage, slot],
            dst_ref=in_face.at[stage, slot],
            send_sem=face_ss.at[stage, slot],
            recv_sem=face_rs.at[stage, slot],
            device_id=target,
            device_id_type=MESH,
        )
        copy.start()
        started.append(copy)
        return copy

    loads[0].wait()

    def factors(x, _):
        unary[x + 1] = q[x].astype(F32)
        return 0

    lax.fori_loop(0, 8, factors, 0, unroll=True)
    copies = []

    def send_from(src, dst, ss, rs, target):
        copy = pltpu.make_async_remote_copy(
            src_ref=src, dst_ref=dst, send_sem=ss, recv_sem=rs, device_id=target, device_id_type=MESH
        )
        copy.start()
        started.append(copy)
        return copy

    for k, (d, e) in enumerate(EDGES):
        near = [7 if f % 2 == 0 else 0 for f in (d, e)]
        if (d // 2, e // 2) == (0, 1):
            line_out[k] = unary[near[0] + 1, pl.ds(near[1] * 8, 8)]
        elif (d // 2, e // 2) == (0, 2):
            line_out[k] = unary[near[0] + 1, pl.ds(near[1], 8, stride=8)]
        else:
            for x in range(8):
                row = pl.ds(near[0] * 8 + near[1], 1)
                line_out[k, pl.ds(x, 1)] = unary[x + 1, row]
    for d in range(6):
        near, behind = (7, 6) if d % 2 == 0 else (0, 1)
        halo_out[d, pl.ds(0, 64)] = layer(unary, d // 2, near).astype(BF16)
        halo_out[d, pl.ds(64, 64)] = layer(unary, d // 2, behind).astype(BF16)
    pl.semaphore_wait(barrier, met)
    for k in reversed(range(len(EDGES))):
        copies.append(send_from(line_out.at[k], line_in.at[k], line_ss.at[k], line_rs.at[k], across[k]))
    for d in reversed(range(6)):
        copies.append(send_from(halo_out.at[d], halo_in.at[d], halo_ss.at[d], halo_rs.at[d], neighbour[d]))

    loads[1].wait()
    factor = jnp.exp(pot[...].astype(F32) / 64.0)
    table[...] = factor.astype(BF16)
    table_t[...] = factor.T.astype(BF16)

    def push(t, d, x, message):
        if d == 0:
            inc[t, d, x + 2] = message
        elif d == 1:
            inc[t, d, x] = message
        elif d == 2:
            inc[t, d, x + 1, pl.ds(8, 56)] = message[:56]
        elif d == 3:
            inc[t, d, x + 1, pl.ds(0, 56)] = message[8:]
        elif d == 4:
            inc[t, d, x + 1] = turn(message, 1)
        else:
            inc[t, d, x + 1] = turn(message, -1)

    def first_messages(x, _):
        value = jnp.exp(unary[x + 1] / 32.0)
        unary[x + 1] = value
        scores = dot(value, table[...])
        inv_total = 1.0 / lanes(scores)
        inv_s1[x + 1] = 1.0 / scores
        inv_t1[x + 1] = wide(inv_total)
        message = scores * (LABELS * inv_total)
        for d in range(6):
            push(0, d, x, message)
        return 0

    lax.fori_loop(0, 8, first_messages, 0, unroll=True)

    for copy in copies:
        copy.wait_recv()
    scores_in = jnp.concatenate(
        [halo_in[...].astype(F32).reshape(768, LABELS), line_in[...].reshape(96, LABELS)], axis=0
    )
    value = jnp.exp(scores_in / 32.0)
    scores = dot(value, table[...])
    inv_total = 1.0 / lanes(scores)
    ghost_u[...] = value
    ghost_is[...] = 1.0 / scores
    ghost_it[...] = wide(inv_total)
    ghost_m[...] = scores * (LABELS * inv_total)
    for d in range(6):
        face = ghost_m[pl.ds(d * 128, 64)]
        put(inc, (0, d), d // 2, d % 2 == 1, jnp.where(outside[d], 1.0, face))

    def line_of(d, e):
        return pl.ds(768 + edge_at(d, e) * 8, 8)

    for d in range(6):
        near = ghost_m[pl.ds(d * 128, 64)]
        value = ghost_u[pl.ds(d * 128, 64)] * ghost_m[pl.ds(d * 128 + 64, 64)]
        p, r = [axis for axis in range(3) if axis != d // 2]
        for e in (2 * p, 2 * p + 1):
            line = jnp.where(outside[e], 1.0, ghost_m[line_of(d, e)])
            if e % 2 == 0:
                value = value * jnp.concatenate([line, near[:56]], axis=0)
            else:
                value = value * jnp.concatenate([near[8:], line], axis=0)
        for e in (2 * r, 2 * r + 1):
            side[d, e % 2] = turn(near, 1 - 2 * (e % 2))
            line = jnp.where(outside[e], 1.0, ghost_m[line_of(d, e)])
            side[d, e % 2, pl.ds(0 if e % 2 == 0 else 7, 8, stride=8)] = line
            value = value * side[d, e % 2]
        ghost_c[pl.ds(d * 64, 64)] = value
    scores = dot(ghost_c[...], table[...])
    inv_total = 1.0 / lanes(scores)
    ghost_is2[...] = 1.0 / scores
    ghost_it2[...] = wide(inv_total)
    ghost_m2 = scores * (LABELS * inv_total)
    for t in (1, 2):
        if t == 2:
            faces = []
            for d in range(6):
                value = take(unary, (), d // 2, d % 2 == 0)
                for e in range(6):
                    if e != d ^ 1:
                        value = value * take(inc, (t - 1, e), d // 2, d % 2 == 0)
                faces.append(value.astype(BF16))
            scores = dot(jnp.concatenate(faces, axis=0), table[...])
            message = scores * (LABELS / lanes(scores))
            copies = [send(0, d, neighbour[d], message[d * 64 : d * 64 + 64]) for d in reversed(range(6))]

        def messages(x, _, t=t):
            values, _ = cavities(unary[x + 1], [inc[t - 1, d, x + 1] for d in range(6)])
            for d in range(6):
                rounded = values[d].astype(BF16)
                cav[t - 1, d, x + 1] = values[d]
                cav16[t - 1, d, x] = rounded
                scores = dot(rounded, table[...])
                inv_total = 1.0 / lanes(scores)
                inv_s[t - 1, d, x + 1] = 1.0 / scores
                inv_t[t - 1, d, x + 1] = wide(inv_total)
                push(t, d, x, scores * (LABELS * inv_total))
            return 0

        lax.fori_loop(0, 8, messages, 0, unroll=True)
        if t == 1:
            for d in range(6):
                face = ghost_m2[d * 64 : d * 64 + 64]
                put(inc, (1, d), d // 2, d % 2 == 1, jnp.where(outside[d], 1.0, face))
    for copy in copies:
        copy.wait_recv()
    for d in range(6):
        face = in_face[0, d].astype(F32)
        put(inc, (2, d), d // 2, d % 2 == 1, jnp.where(outside[d], 1.0, face))

    loads[2].wait()
    empty = jnp.zeros((64, LABELS), F32)
    for x in (0, 9):
        log_grad[x] = empty
        for t in range(2):
            whole[t, x] = empty
            for d in range(6):
                parts[t, d, x] = empty

    def beliefs(x, _):
        product = unary[x + 1]
        for d in range(6):
            product = product * inc[2, d, x + 1]
        target = bg[x].astype(F32)
        log_grad[x + 1] = target - product * (lanes(target) / lanes(product))
        return 0

    lax.fori_loop(0, 8, beliefs, 0, unroll=True)
    copies = [send(1, d, neighbour[d ^ 1], take(log_grad, (), d // 2, d % 2 == 1)) for d in reversed(range(6))]

    place = lax.rem(lax.broadcasted_iota(jnp.int32, (64, LABELS), 0), 8)
    border = jnp.zeros((8, LABELS), F32)

    def arrived(read, d, x):
        if d == 0:
            return read(d, x + 2)
        if d == 1:
            return read(d, x)
        if d == 2:
            return jnp.concatenate([read(d, x + 1)[8:], border], axis=0)
        if d == 3:
            return jnp.concatenate([border, read(d, x + 1)[:56]], axis=0)
        if d == 4:
            return jnp.where(place == 7, 0.0, turn(read(d, x + 1), -1))
        return jnp.where(place == 0, 0.0, turn(read(d, x + 1), 1))

    def last_grads(d, x):
        return log_grad[x]

    def grads_of(t):
        return lambda d, x: whole[t, x] - parts[t, d ^ 1, x]

    pair[...] = jnp.zeros_like(pair)

    def backward(t, read):
        for x in range(8):
            total = None
            for d in range(6):
                grad = arrived(read, d, x)
                score_grad = grad * inv_s[t, d, x + 1] - lanes(grad) * inv_t[t, d, x + 1]
                rounded = score_grad.astype(BF16)
                sgrad16[d, x] = rounded
                part = dot(rounded, table_t[...]) * cav[t, d, x + 1]
                parts[t, d, x + 1] = part
                total = part if total is None else total + part
            whole[t, x + 1] = total
        for d in range(6):
            pair[...] += dot_rows(
                cav16[t, d].reshape(512, LABELS), sgrad16[d].reshape(512, LABELS)
            )

    def backward_faces(t, stage):
        rounded, at = [], []
        for d in range(6):
            upper = d % 2 == 0
            grad = jnp.where(outside[d ^ 1], 0.0, in_face[stage, d].astype(F32))
            score_grad = grad * take(inv_s, (t, d), d // 2, upper)
            score_grad -= lanes(grad) * take(inv_t, (t, d), d // 2, upper)
            rounded.append(score_grad.astype(BF16))
            at.append(take(cav, (t, d), d // 2, upper))
        rounded = jnp.concatenate(rounded, axis=0)
        back = dot(rounded, table_t[...])
        for d in range(6):
            upper = d % 2 == 0
            part = back[d * 64 : d * 64 + 64] * at[d]
            put(parts, (t, d), d // 2, upper, part)
            put(whole, (t,), d // 2, upper, take(whole, (t,), d // 2, upper) + part)
        return at, rounded

    def leaving(t):
        return [
            take(whole, (t,), d // 2, d % 2 == 1) - take(parts, (t, d ^ 1), d // 2, d % 2 == 1)
            for d in range(6)
        ]

    backward(1, last_grads)
    for copy in copies:
        copy.wait_recv()
    at, rounded = backward_faces(1, 1)
    edge = leaving(1)
    copies = [send(2, d, neighbour[d ^ 1], edge[d]) for d in range(6)]
    pair[...] += dot_rows(jnp.concatenate(at, axis=0).astype(BF16), rounded)

    grad = jnp.concatenate([jnp.where(outside[d], 0.0, edge[d]) for d in range(6)], axis=0)
    score_grad = grad * ghost_is2[...] - lanes(grad) * ghost_it2[...]
    rounded = score_grad.astype(BF16)
    pair[...] += dot_rows(ghost_c[...].astype(BF16), rounded)
    beyond = dot(rounded, table_t[...]) * ghost_c[...]

    backward(0, grads_of(1))

    read = grads_of(0)

    def first_grad(x):
        grad = arrived(read, 0, x)
        for d in range(1, 6):
            grad += arrived(read, d, x)
        score_grad = grad * inv_s1[x + 1] - lanes(grad) * inv_t1[x + 1]
        return score_grad.astype(BF16)

    for x in range(8):
        sgrad16[0, x] = first_grad(x)
        cav16[0, 0, x] = unary[x + 1].astype(BF16)
    pair[...] += dot_rows(cav16[0, 0].reshape(512, LABELS), sgrad16[0].reshape(512, LABELS))

    edge = leaving(0)
    lines = [None] * len(EDGES)

    def add_line(d, e, value):
        k = edge_at(d, e)
        value = jnp.where(outside[e], 0.0, value)
        lines[k] = value if lines[k] is None else lines[k] + value

    for d in range(6):
        here = beyond[d * 64 : d * 64 + 64]
        near = jnp.where(outside[d], 0.0, edge[d])
        p, r = [axis for axis in range(3) if axis != d // 2]
        near += jnp.concatenate([here[8:], border], axis=0)
        add_line(d, 2 * p, here[:8])
        near += jnp.concatenate([border, here[:56]], axis=0)
        add_line(d, 2 * p + 1, here[56:])
        near += jnp.where(place == 7, 0.0, turn(here, -1))
        near += jnp.where(place == 0, 0.0, turn(here, 1))
        side[d, 0] = here
        add_line(d, 2 * r, side[d, 0, pl.ds(0, 8, stride=8)])
        add_line(d, 2 * r + 1, side[d, 0, pl.ds(7, 8, stride=8)])
        ghost_g[pl.ds(d * 128, 64)] = near
        ghost_g[pl.ds(d * 128 + 64, 64)] = here
    for k in range(len(EDGES)):
        ghost_g[pl.ds(768 + k * 8, 8)] = lines[k]
    grad = ghost_g[...]
    score_grad = grad * ghost_is[...] - lanes(grad) * ghost_it[...]
    pair[...] += dot_rows(ghost_u[...].astype(BF16), score_grad.astype(BF16))

    height = LABELS // firsts

    def rows_of(j):
        return pl.ds(pl.multiple_of(j * height, height), height)

    sends = [
        send_from(pair.at[rows_of(j)], part1.at[k], s1_ss.at[k], s1_rs.at[k], target)
        for k, (target, j) in enumerate(first_peers)
    ]

    for copy in copies:
        copy.wait_recv()
    backward_faces(0, 2)
    edge = leaving(0)
    copies = [send(3, d, neighbour[d ^ 1], edge[d]) for d in range(6)]

    for copy in sends:
        copy.wait_recv()
    mine = pair[rows_of(first_id)]
    for k in range(1, firsts):
        mine += part1[k - 1]
    part2[second_id] = mine.astype(BF16)
    own = part2.at[second_id]
    early = list(started)
    sends = [
        send_from(own, own, s2_ss.at[k], s2_rs.at[k], target)
        for k, target in enumerate(second_peers)
    ]
    for x in range(8):
        back = dot(first_grad(x), table_t[...]) * unary[x + 1]
        ug[x + 1] = log_grad[x + 1] + whole[1, x + 1] + whole[0, x + 1] + back
    for copy in copies:
        copy.wait_recv()
    rounded = []
    for d in range(6):
        upper = d % 2 == 0
        grad = jnp.where(outside[d ^ 1], 0.0, in_face[3, d].astype(F32))
        score_grad = grad * take(inv_s1, (), d // 2, upper)
        score_grad -= lanes(grad) * take(inv_t1, (), d // 2, upper)
        rounded.append(score_grad.astype(BF16))
    back = dot(jnp.concatenate(rounded, axis=0), table_t[...])
    for d in range(6):
        upper = d % 2 == 0
        part = back[d * 64 : d * 64 + 64] * take(unary, (), d // 2, upper)
        put(ug, (), d // 2, upper, take(ug, (), d // 2, upper) + part)
    store = pltpu.make_async_copy(ug.at[pl.ds(1, 8)], ug_out, out_sem.at[0])
    store.start()
    for copy in early:
        copy.wait_send()
    factor = jnp.exp(pot[...].astype(F32) / 64.0) * (LABELS / math.sqrt(CELLS))

    for copy in sends:
        copy.wait_recv()
    final[rows_of(first_id)] = jnp.sum(part2[...].astype(F32), axis=0)
    here = final.at[rows_of(first_id)]
    gathers = [
        send_from(here, here, s3_ss.at[k], s3_rs.at[k], target)
        for k, (target, _) in enumerate(first_peers)
    ]
    for copy in sends:
        copy.wait_send()
    for copy in gathers:
        copy.wait_recv()
    pair[...] = factor * final[...]
    store2 = pltpu.make_async_copy(pair, pg_out, out_sem.at[1])
    store2.start()
    for copy in gathers:
        copy.wait_send()
    store.wait()
    store2.wait()


def finish(ug, pg, ug_out, pg_out, ug_held, pg_held, sem):
    moves = [(pg, pg_held, pg_out)]
    for x in range(0, 8, 4):
        part = pl.ds(x, 4)
        moves.append((ug.at[part], ug_held.at[part], ug_out.at[part]))
    loads = [pltpu.make_async_copy(a, b, sem.at[0, k]) for k, (a, b, c) in enumerate(moves)]
    stores = [pltpu.make_async_copy(b, c, sem.at[1, k]) for k, (a, b, c) in enumerate(moves)]
    for load in loads:
        load.start()
    for load, store in zip(loads, stores):
        load.wait()
        store.start()
    for store in stores:
        store.wait()


def on_device(unary_q, potential_q, belief_grad):
    slabs = (8, 64, LABELS)
    padded = (10, 64, LABELS)
    firsts = lax.axis_size("gx") * 2
    seconds = lax.axis_size("gy") * (lax.axis_size("gz") // 2)
    height = LABELS // firsts
    vmem, dma = pltpu.VMEM, pltpu.SemaphoreType.DMA
    unary_grad, potential_grad = pl.pallas_call(
        kernel,
        out_shape=(
            jax.ShapeDtypeStruct(slabs, F32),
            jax.ShapeDtypeStruct((LABELS, LABELS), F32),
        ),
        in_specs=[pl.BlockSpec(memory_space=pltpu.HBM)] * 3,
        out_specs=(pl.BlockSpec(memory_space=pltpu.HBM),) * 2,
        scratch_shapes=[
            vmem(slabs, jnp.int32),
            vmem((LABELS, LABELS), jnp.int32),
            vmem(slabs, BF16),
            vmem((LABELS, LABELS), BF16),
            vmem((LABELS, LABELS), BF16),
            vmem(padded, F32),
            vmem((3, 6, *padded), F32),
            vmem((2, 6, *padded), F32),
            vmem((2, 6, *slabs), BF16),
            vmem((2, 6, *padded), F32),
            vmem((2, 6, *padded), F32),
            vmem(padded, F32),
            vmem(padded, F32),
            vmem(padded, F32),
            vmem((2, 6, *padded), F32),
            vmem((2, *padded), F32),
            vmem((6, *slabs), BF16),
            vmem((LABELS, LABELS), F32),
            vmem(padded, F32),
            vmem((4, 6, 64, LABELS), BF16),
            vmem((4, 6, 64, LABELS), BF16),
            *[vmem((GHOSTS, LABELS), F32)] * 5,
            *[vmem((384, LABELS), F32)] * 3,
            vmem((6, 2, 64, LABELS), F32),
            vmem((len(EDGES), 8, LABELS), F32),
            vmem((len(EDGES), 8, LABELS), F32),
            vmem((6, 128, LABELS), BF16),
            vmem((6, 128, LABELS), BF16),
            vmem((firsts - 1, height, LABELS), F32),
            vmem((seconds, height, LABELS), BF16),
            vmem((LABELS, LABELS), F32),
            dma((3,)),
            dma((2,)),
            dma((4, 6)),
            dma((4, 6)),
            dma((6,)),
            dma((6,)),
            dma((len(EDGES),)),
            dma((len(EDGES),)),
            dma((firsts - 1,)),
            dma((firsts - 1,)),
            dma((seconds - 1,)),
            dma((seconds - 1,)),
            dma((firsts - 1,)),
            dma((firsts - 1,)),
        ],
        compiler_params=pltpu.CompilerParams(
            collective_id=0, has_side_effects=True, vmem_limit_bytes=60 * 2**20
        ),
    )(unary_q.reshape(slabs), potential_q, belief_grad.reshape(slabs))
    unary_grad, potential_grad = pl.pallas_call(
        finish,
        out_shape=(
            jax.ShapeDtypeStruct(slabs, F32),
            jax.ShapeDtypeStruct((LABELS, LABELS), F32),
        ),
        in_specs=[pl.BlockSpec(memory_space=pltpu.HBM)] * 2,
        out_specs=(pl.BlockSpec(memory_space=pltpu.HBM),) * 2,
        scratch_shapes=[vmem(slabs, F32), vmem((LABELS, LABELS), F32), dma((2, 3))],
    )(unary_grad, potential_grad)
    return unary_grad.reshape(unary_q.shape), potential_grad


def solution(mesh):
    return jax.shard_map(
        on_device,
        mesh=mesh,
        in_specs=(P("gx", "gy", "gz", None), P(), P("gx", "gy", "gz", None)),
        out_specs=(P("gx", "gy", "gz", None), P()),
        check_vma=False,
    )
```
